256 devices in a mesh: dp: 32 (over x_hi, z, core), blk: 8 (over x_lo, y).
Axes of the slice: x: 4 (x_hi: 2, x_lo: 2; x = x_hi * 2 + x_lo), y: 4, z: 8, core: 2. Of those that a mesh axis runs over, the one named last changes fastest.
Arguments:
- attn_cols: bfloat16 [32768, 7168], P('blk', 'dp'), may hold values from -6 to 6
- residual: bfloat16 [32768, 7168], P(('blk', 'dp')), may hold values from -80 to 80
- norm_gain: bfloat16 [7168], replicated, may hold values from 0.5 to 1.5
- router_weight: bfloat16 [7168, 32], replicated, may hold values from -0.0625 to 0.0625
- expert_ids: int32 [32768, 2], P(('blk', 'dp')), may hold values from 0 to 31, all different within a row; in each aligned block of 128 rows (0 to 127, 128 to 255, ...) at most 10 rows name the same one
- gate_weight: bfloat16 [32, 7168, 1024], P('dp', None, 'blk'), may hold values from -0.0625 to 0.0625
- up_weight: bfloat16 [32, 7168, 1024], P('dp', None, 'blk'), may hold values from -0.0625 to 0.0625
- down_weight: bfloat16 [32, 7168, 1024], P('dp', 'blk'), may hold values from -0.1875 to 0.1875
Outputs:
- layer_out: bfloat16 [32768, 7168], P(('blk', 'dp'))
The draws below stay inside these ranges and needn't reach their ends.
Inputs may be any that keep to these rules, and one draw needn't show every extreme that they name: `expert_ids`: within each aligned block of 128 rows (the rows of one device) no expert is named by more than 10 rows, and in some block some expert is named by exactly 10 rows; the 2 experts of a row differ.
All inputs are finite; a program needn't handle non-finite values.
Results may differ from the reference program's by a relative error of at most 0.0044.
Values may be sent and summed in bfloat16 or wider, within the bound.
A program may use at most 192 MiB of HBM per device.

```python
import math
import jax
import jax.numpy as jnp
import numpy as np
from jax import lax

D = 7168
FF = 1024
TOP = 2
TOK_DEV = 128
EXPERTS = 32
CAP = 10
TOKENS = 32768


def draw_residual(key, part):
    key = jax.random.fold_in(key, 7)
    first, second, third = jax.random.split(key, 3)
    rowscale = jnp.exp(jax.random.uniform(first, (TOKENS, 1)) * math.log(10.0)) / math.sqrt(10.0)
    base = jnp.clip(jax.random.normal(third, (TOKENS, D)), -4.0, 4.0)
    colscale = jnp.exp(jax.random.uniform(second, (1, D)) * math.log(10.0)) / math.sqrt(10.0)
    return (base * rowscale * colscale).astype(jnp.bfloat16)


def level_of(own_key, extent, cuts, least, largest):
    def one(dim, parts):
        heights = jax.random.uniform(jax.random.fold_in(jax.random.fold_in(own_key, 6), dim), (parts,), jnp.float32, least / len(cuts), largest / len(cuts))
        return jnp.repeat(jnp.exp(heights), extent[dim] // parts).reshape((-1,) + (1,) * (len(extent) - dim - 1))

    level = one(*cuts[0])
    for cut in cuts[1:]:
        level = level * one(*cut)
    return level


def assign_block(own_key, own, number, rows, amount, top, limit, lean):
    order = jax.random.permutation(own_key, amount)
    packed, common = load_shares(amount, rows * top, limit, lean, True), load_shares(amount, rows * top, limit, lean, False)
    places = jnp.arange(amount)

    def named(sizes, turn):
        used = int((sizes > 0).sum())
        fixed = max(1, used // 4)
        shifted = fixed + (places - fixed + turn * (used - fixed)) % max(1, amount - fixed)
        return jnp.zeros((amount,), jnp.int32).at[order[jnp.where(places < fixed, places, shifted)]].set(jnp.asarray(sizes, jnp.int32))

    sizes = jnp.where(number % 4 == 0, named(packed, number // 4), named(common, number - number // 4 - 1))
    mixed = jax.random.permutation(jax.random.fold_in(own, 3), amount)
    donor, taker = mixed[0:amount // 2 * 2:2], mixed[1:amount // 2 * 2:2]
    margin = jnp.minimum(sizes[donor] - 1, limit - sizes[taker]) // 2
    margin = jnp.where((donor == order[0]) | (taker == order[0]) | (sizes[taker] == 0), 0, jnp.maximum(margin, 0))
    shifted = jax.random.randint(jax.random.fold_in(own, 4), (amount // 2,), 0, 1 << 20) % (margin + 1)
    sizes = sizes.at[donor].add(-shifted).at[taker].add(shifted)
    members = jnp.searchsorted(jnp.cumsum(sizes), jnp.arange(rows * top), side="right").astype(jnp.int32)
    listing = members.reshape(top, rows).T
    listing = listing[jax.random.permutation(jax.random.fold_in(own, 1), rows)]
    turn = jax.random.randint(jax.random.fold_in(own, 2), (rows, 1), 0, top)
    return jnp.take_along_axis(listing, (jnp.arange(top)[None, :] + turn) % top, axis=1)


def load_shares(count, total, bound, skew, full):
    loads = [(1 << 20) // math.isqrt(standing ** skew) + 1 for standing in range(1, count + 1)]
    largest = bound if full else min(bound, max(-(-total // count), total * loads[0] // sum(loads)))
    least = 1 if total - largest >= count - 1 else 0
    counts, spare = [largest] + [least] * (count - 1), total - largest - least * (count - 1)
    while spare > 0:
        candidates = [i for i in range(1, count) if counts[i] < largest] or [i for i in range(1, count) if counts[i] < bound]
        pool, remaining = sum([loads[i] for i in candidates]), spare
        for i in candidates:
            more = min(bound - counts[i], max(1, remaining * loads[i] // pool), spare)
            counts[i] = counts[i] + more
            spare = spare - more
    return np.array(counts)


def noise(own_key, extent, scale, bound, pieces=(), held_as=jnp.bfloat16):
    array = scale * jax.random.normal(own_key, extent, jnp.float32)
    if pieces:
        array = array * level_of(own_key, extent, pieces, -0.22, 0.18)
    return jnp.clip(array, -bound, bound).astype(held_as)


def setup_inputs(seed: int = 0) -> dict:
    arg_keys = jax.random.split(jax.random.key(seed), 9)
    attn_cols = noise(arg_keys[0], (TOKENS, D), 1.0, 6.0, ((0, 8), (1, 32)))
    residual = draw_residual(jax.random.fold_in(arg_keys[8], 71), 0)
    norm_gain = jnp.clip(1.0 + 0.1 * jax.random.normal(arg_keys[2], (D,), jnp.float32), 0.5, 1.5).astype(jnp.bfloat16)
    router_weight = noise(arg_keys[3], (D, EXPERTS), D ** -0.5, 0.0625)
    expert_ids_keys = jax.random.split(jax.random.fold_in(arg_keys[4], 1), TOKENS // TOK_DEV)
    expert_ids_turns = jax.random.permutation(jax.random.fold_in(arg_keys[4], 3), TOKENS // TOK_DEV)
    expert_ids = jax.vmap(lambda own, number: assign_block(jax.random.fold_in(arg_keys[4], 2), own, number, TOK_DEV, EXPERTS, TOP, CAP, 1))(expert_ids_keys, expert_ids_turns).reshape((TOKENS, TOP))
    gate_weight = noise(arg_keys[5], (EXPERTS, D, FF), D ** -0.5, 0.0625, ((0, 32), (2, 8)))
    up_weight = noise(arg_keys[6], (EXPERTS, D, FF), D ** -0.5, 0.0625, ((0, 32), (2, 8)))
    down_weight = noise(arg_keys[7], (EXPERTS, D, FF), FF ** -0.5, 0.1875, ((0, 32), (1, 8)))
    return {"attn_cols": attn_cols, "residual": residual, "norm_gain": norm_gain, "router_weight": router_weight, "expert_ids": expert_ids, "gate_weight": gate_weight, "up_weight": up_weight, "down_weight": down_weight}


def expert_ffn(rows, gate_one, up_one, down_one):
    gated = jnp.dot(rows, gate_one, preferred_element_type=jnp.float32)
    upward = jnp.dot(rows, up_one, preferred_element_type=jnp.float32)
    hidden = (jax.nn.silu(gated) * upward).astype(jnp.bfloat16)
    return jnp.dot(hidden, down_one.T, preferred_element_type=jnp.float32).astype(jnp.bfloat16)

def reference(attn_cols, residual, norm_gain, router_weight, expert_ids, gate_weight, up_weight, down_weight):
    stream = residual.astype(jnp.float32) + attn_cols.astype(jnp.float32)
    meansq = lax.optimization_barrier(jnp.mean(stream * stream, axis=1, keepdims=True))
    normed = (stream * lax.rsqrt(meansq + 1e-06) * norm_gain.astype(jnp.float32)).astype(jnp.bfloat16)
    affinity = jax.nn.sigmoid(jnp.dot(normed, router_weight, preferred_element_type=jnp.float32))
    chosen = jnp.take_along_axis(affinity, expert_ids, axis=1)
    weights = 2.5 * chosen / lax.optimization_barrier(jnp.sum(chosen, axis=1, keepdims=True))
    devices = TOKENS // TOK_DEV
    flat_ids = expert_ids.reshape(devices, TOK_DEV * TOP)
    onehot = (flat_ids[:, :, None] == jnp.arange(EXPERTS, dtype=jnp.int32)[None, None, :]).astype(jnp.int32)
    before = jnp.cumsum(onehot, axis=1) - onehot
    ranks = lax.optimization_barrier(jnp.sum(before * onehot, axis=2)).astype(jnp.int32)
    slots = (flat_ids * CAP + ranks).astype(jnp.int32)
    dev_index = jnp.arange(devices, dtype=jnp.int32)[:, None]
    owner_tok = (dev_index * TOK_DEV + jnp.arange(TOK_DEV * TOP, dtype=jnp.int32)[None, :] // TOP).astype(jnp.int32)
    table = jnp.full((devices, EXPERTS * CAP), TOKENS, dtype=jnp.int32)
    table = table.at[jnp.broadcast_to(dev_index, slots.shape), slots].set(owner_tok)
    table = table.reshape(devices, EXPERTS, CAP).transpose(1, 0, 2).reshape(EXPERTS, devices * CAP)
    padded = jnp.concatenate([normed, jnp.zeros((1, D), normed.dtype)], axis=0)

    def one_expert(inputs):
        row_index, gate_one, up_one, down_one = inputs
        return expert_ffn(padded[row_index], gate_one, up_one, down_one)
    outputs = lax.map(one_expert, (table, gate_weight, up_weight, down_weight))
    row_pos = (dev_index * CAP + ranks).astype(jnp.int32)
    picked = outputs[flat_ids, row_pos].reshape(TOKENS, TOP, D)
    summed = stream
    for member in range(TOP):
        summed = summed + weights[:, member:member + 1] * picked[:, member].astype(jnp.float32)
    return summed.astype(jnp.bfloat16)
```

```python
import jax
import jax.numpy as jnp
from jax import lax
from jax.experimental import pallas as pl
from jax.experimental.pallas import tpu as pltpu
from jax.sharding import PartitionSpec as P

BF = jnp.bfloat16
F32 = jnp.float32
I32 = jnp.int32
D = 7168
FF = 1024
TOK = 128
EXPERTS = 32
CAP = 10
SLOTS = EXPERTS * CAP
PIECE = 224
CHUNK = 896
HALF = D // 2
UNIT = 256
BACK = 144
MESH = pl.DeviceIdType.MESH


def div(a, n):
    return lax.div(a, jnp.int32(n))


def rem(a, n):
    return lax.rem(a, jnp.int32(n))


def shifted(d, k, sign):
    x = rem(div(d, 16) + k // 16, 2)
    z = rem(rem(div(d, 2), 8) + (sign * ((k // 2) % 8) + 8), 8)
    c = rem(rem(d, 2) + k % 2, 2)
    return x * 16 + z * 2 + c


def swap_rows(rows, cols):
    r = lax.broadcasted_iota(I32, (rows, 128), 0)
    outer = lax.shift_right_logical(r * 26215, 21)
    inner = r - outer * 80
    mid = lax.shift_right_logical(inner * 6554, 16)
    last = inner - mid * CAP
    return outer, mid, last, r


def kernel(
    attn,
    residual,
    gain,
    router,
    ids,
    pos,
    pos_t,
    gate,
    up,
    down,
    out,
    gate_all,
    up_all,
    down_all,
    cols,
    stream,
    normed,
    perm,
    perm_back,
    perm_home,
    stack,
    outgoing,
    arrived,
    rows,
    wbuf,
    dbuf,
    acc,
    hidden,
    pile,
    returned,
    coef,
    s_attn,
    r_attn,
    s_ring,
    r_ring,
    s_disp,
    r_disp,
    s_fwd,
    r_fwd,
    s_hid,
    r_hid,
    s_ret,
    r_ret,
    l_sem,
    w_sem,
):
    d = lax.axis_index("dp")
    b = lax.axis_index("blk")
    other = rem(b + 4, 8)
    half = div(b, 4)
    y = rem(b, 4)
    ring_r = half * 4 + rem(y + 1, 4)
    ring_l = half * 4 + rem(y + 3, 4)

    def remote(src, dst, ss, rs, dev):
        return pltpu.make_async_remote_copy(
            src_ref=src,
            dst_ref=dst,
            send_sem=ss,
            recv_sem=rs,
            device_id=dev,
            device_id_type=MESH,
        )

    barrier = pltpu.get_barrier_semaphore()
    for k in range(EXPERTS):
        p = shifted(d, k, 1)
        for q in (b, other):
            if k == 0 and q is b:
                continue
            pl.semaphore_signal(barrier, inc=1, device_id=(p, q), device_id_type=MESH)
    for q in (ring_l, ring_r):
        pl.semaphore_signal(barrier, inc=1, device_id=(d, q), device_id_type=MESH)
    pl.semaphore_wait(barrier, 65)

    attn_out = []
    for k in range(1, 32):
        p = shifted(d, k, 1)
        c = remote(
            attn.at[pl.ds(pl.multiple_of(p * TOK, TOK), TOK)],
            cols.at[d],
            s_attn.at[k],
            r_attn.at[k],
            (p, b),
        )
        c.start()
        attn_out.append(c)
    own_cols = pltpu.make_async_copy(
        attn.at[pl.ds(pl.multiple_of(d * TOK, TOK), TOK)], cols.at[d], l_sem.at[0]
    )
    own_cols.start()
    own_res = pltpu.make_async_copy(residual, normed, l_sem.at[1])
    own_res.start()

    mine = (gate.at[0], up.at[0], down.at[0])
    gathered = (gate_all, up_all, down_all)
    first = []
    for a in range(3):
        c0 = remote(mine[a], gathered[a].at[0], s_ring.at[a, 0], r_ring.at[a, 0], (d, ring_r))
        c1 = remote(mine[a], gathered[a].at[1], s_ring.at[a, 1], r_ring.at[a, 1], (d, ring_l))
        c0.start()
        c1.start()
        first.append((c0, c1))
    second = []

    def pass_on(a):
        n = gathered[a].shape[1] // 2
        c0, c1 = first[a]
        c0.wait_recv()
        f0 = remote(
            gathered[a].at[0, pl.ds(0, n)],
            gathered[a].at[2, pl.ds(0, n)],
            s_ring.at[a, 2],
            r_ring.at[a, 2],
            (d, ring_r),
        )
        f0.start()
        c1.wait_recv()
        f1 = remote(
            gathered[a].at[1, pl.ds(n, n)],
            gathered[a].at[2, pl.ds(n, n)],
            s_ring.at[a, 3],
            r_ring.at[a, 3],
            (d, ring_l),
        )
        f1.start()
        second.append((f0, f1))

    def fetch_in(slot):
        src = mine if slot == 0 else (gate_all.at[slot - 1], up_all.at[slot - 1])
        s = slot % 2
        cs = []
        for i in range(2):
            c = pltpu.make_async_copy(
                src[i], wbuf.at[s, :, pl.ds(i * 128, 128)], w_sem.at[s, i]
            )
            c.start()
            cs.append(c)
        return cs

    def fetch_out(slot):
        src = down.at[0] if slot == 0 else down_all.at[slot - 1]
        s = slot % 2
        c = pltpu.make_async_copy(src, dbuf.at[s], w_sem.at[s, 2])
        c.start()
        return c

    in_copies = {0: fetch_in(0)}
    out_copies = {0: fetch_out(0)}

    outer, mid, last, r = swap_rows(640, 640)
    col = mid * 80 + outer * CAP + last
    lane = lax.broadcasted_iota(I32, (640, 128), 1)
    for j in range(5):
        perm[:, j * 128 : (j + 1) * 128] = jnp.where(lane + j * 128 == col, 1.0, 0.0).astype(BF)
    r = lax.broadcasted_iota(I32, (1152, 128), 0)
    outer = lax.shift_right_logical(r * 14564, 21)
    inner = r - outer * BACK
    mid = lax.shift_right_logical(inner * 6554, 16)
    last = inner - mid * CAP
    col = jnp.where(inner < 140, mid * 80 + outer * CAP + last, -1)
    lane = lax.broadcasted_iota(I32, (1152, 128), 1)
    for j in range(9):
        perm_back[:, j * 128 : (j + 1) * 128] = jnp.where(lane + j * 128 == col, 1.0, 0.0).astype(
            BF
        )
    outer, mid, last, r = swap_rows(1120, 1152)
    col = mid * BACK + outer * CAP + last
    lane = lax.broadcasted_iota(I32, (1120, 128), 1)
    for j in range(9):
        perm_home[:, j * 128 : (j + 1) * 128] = jnp.where(lane + j * 128 == col, 1.0, 0.0).astype(
            BF
        )
    stack_tail = jnp.zeros((32, UNIT), BF)

    for c in attn_out:
        c.wait_recv()
    own_cols.wait()
    own_res.wait()

    def norm_rows(i, carry):
        rs = pl.ds(pl.multiple_of(i * 32, 32), 32)
        total = jnp.zeros((32, 1), F32)
        for q in range(8):
            sl = slice(q * CHUNK, (q + 1) * CHUNK)
            joined = jnp.concatenate([cols[4 * q + m, rs, :] for m in range(4)], axis=1)
            s = normed[rs, sl].astype(F32) + joined.astype(F32)
            stream[rs, sl] = s
            total += jnp.sum(s * s, axis=1, keepdims=True)
        inv = lax.rsqrt(total * (1.0 / D) + 1e-06)
        for q in range(8):
            sl = slice(q * CHUNK, (q + 1) * CHUNK)
            normed[rs, sl] = (stream[rs, sl] * inv * gain[:, sl].astype(F32)).astype(BF)
        return carry

    lax.fori_loop(0, 4, norm_rows, 0)

    def disp_copy(k):
        return remote(
            outgoing.at[pl.ds(pl.multiple_of(k * 80, 80), 80)],
            arrived.at[0, pl.ds(pl.multiple_of(k * 80, 80), 80)],
            s_disp.at[k],
            r_disp.at[k],
            (shifted(d, k, 1), jnp.where(k < 16, b, other)),
        )

    def pick(g):
        want = lax.broadcasted_iota(I32, (80, TOK), 0) + g * 80
        hit = jnp.logical_or(want == pos_t[0:1, :], want == pos_t[1:2, :])
        one = jnp.where(hit, 1.0, 0.0).astype(BF)
        for j in range(8):
            stack[j * 80 : (j + 1) * 80, :] = jnp.dot(
                one, normed[:, j * CHUNK : (j + 1) * CHUNK], preferred_element_type=F32
            ).astype(BF)
        outgoing[pl.ds(pl.multiple_of(g * 640, 640), 640), :] = jnp.dot(
            perm[...], stack[...], preferred_element_type=F32
        ).astype(BF)

    def dispatch(g, carry):
        pick(g)
        for i in range(8):
            k = g * 8 + i

            @pl.when(k > 0)
            def _():
                disp_copy(k).start()

        return carry

    lax.fori_loop(0, 4, dispatch, 0)
    own_rows = pltpu.make_async_copy(
        outgoing.at[pl.ds(0, 80)], arrived.at[0, pl.ds(0, 80)], l_sem.at[2]
    )
    own_rows.start()
    pass_on(0)

    logits = jnp.zeros((TOK, EXPERTS), F32)
    for q in range(8):
        sl = slice(q * CHUNK, (q + 1) * CHUNK)
        logits += jnp.dot(normed[:, sl], router[sl, :], preferred_element_type=F32)
    affinity = jax.nn.sigmoid(logits)
    names = lax.broadcasted_iota(I32, (TOK, EXPERTS), 1)
    chosen = [
        jnp.sum(jnp.where(names == ids[:, m : m + 1], affinity, 0.0), axis=1, keepdims=True)
        for m in range(2)
    ]
    scale = 2.5 / (chosen[0] + chosen[1])
    where = lax.broadcasted_iota(I32, (TOK, SLOTS), 1)
    full = jnp.where(where == pos[:, 0:1], chosen[0] * scale, 0.0) + jnp.where(
        where == pos[:, 1:2], chosen[1] * scale, 0.0
    )
    high = full.astype(BF)
    coef[0:TOK, :] = high
    coef[TOK : 2 * TOK, :] = (full - high.astype(F32)).astype(BF)

    def fwd_copy(k):
        sl = pl.ds(pl.multiple_of(k * 80, 80), 80)
        return remote(arrived.at[0, sl], arrived.at[1, sl], s_fwd.at[k], r_fwd.at[k], (d, other))

    def spread(side, g):
        z = jnp.dot(
            perm[...],
            arrived[side, pl.ds(pl.multiple_of(g * 640, 640), 640), :],
            preferred_element_type=F32,
        ).astype(BF)
        for j in range(8):
            rows[
                pl.ds(pl.multiple_of(side * SLOTS + g * 80, 80), 80),
                j * CHUNK : (j + 1) * CHUNK,
            ] = z[j * 80 : (j + 1) * 80, :]

    own_rows.wait()

    def arrive(g, carry):
        for i in range(8):
            k = g * 8 + i

            @pl.when(k > 0)
            def _():
                disp_copy(k).wait_recv()

            fwd_copy(k).start()
        spread(0, g)
        return carry

    def arrive_other(g, carry):
        for i in range(8):
            fwd_copy(g * 8 + i).wait_recv()
        spread(1, g)
        return carry

    lax.fori_loop(0, 2, arrive, 0)
    pass_on(1)
    in_copies[1] = fetch_in(1)
    lax.fori_loop(2, 3, arrive, 0)
    pass_on(2)
    lax.fori_loop(3, 4, arrive, 0)
    lax.fori_loop(0, 4, arrive_other, 0)

    shard_of = (y, rem(y + 3, 4), rem(y + 1, 4), rem(y + 2, 4))
    for slot in range(4):
        for c in in_copies[slot]:
            c.wait()

        def step(i, carry, slot=slot):
            ks = pl.ds(pl.multiple_of(i * 1024, 1024), 1024)
            part = jnp.dot(rows[:, ks], wbuf[slot % 2, ks, :], preferred_element_type=F32)

            @pl.when(i == 0)
            def _():
                acc[...] = part

            @pl.when(i > 0)
            def _():
                acc[...] += part

            return carry

        lax.fori_loop(0, 7, step, 0)
        g = acc[:, 0:128]
        h = (g / (1.0 + jnp.exp(-g)) * acc[:, 128:256]).astype(BF)
        hidden[0, :, pl.ds(pl.multiple_of(shard_of[slot] * 128, 128), 128)] = h
        if slot + 2 < 4:
            n = slot + 2
            if n == 3:
                for a in range(2):
                    first_r = second[a]
                    first_r[0].wait_recv()
                    first_r[1].wait_recv()
            in_copies[n] = fetch_in(n)
    hid = []
    for i in range(2):
        c = remote(
            hidden.at[0, pl.ds(i * SLOTS, SLOTS)],
            hidden.at[1, pl.ds((1 - i) * SLOTS, SLOTS)],
            s_hid.at[i],
            r_hid.at[1 - i],
            (d, other),
        )
        c.start()
        hid.append(c)
    out_copies[1] = fetch_out(1)
    for c in hid:
        c.wait_recv()

    far = 1 - half
    for slot in range(4):
        out_copies[slot].wait()
        for side in range(2):
            rs = slice(side * SLOTS, (side + 1) * SLOTS)
            res = jnp.zeros((SLOTS, CHUNK), F32)
            for part, at in ((0, half), (1, far)):
                res += lax.dot_general(
                    hidden[part, rs, :],
                    dbuf[slot % 2, :, pl.ds(pl.multiple_of(at * 512, 512), 512)],
                    (((1,), (1,)), ((), ())),
                    preferred_element_type=F32,
                )
            at = pl.multiple_of(shard_of[slot] * CHUNK + side * HALF, 128)
            rows[SLOTS : 2 * SLOTS, pl.ds(at, CHUNK)] = res.astype(BF)
        if slot + 2 < 4:
            if slot + 2 == 3:
                second[2][0].wait_recv()
                second[2][1].wait_recv()
            out_copies[slot + 2] = fetch_out(slot + 2)

    def ret_copy(side, k):
        sl = pl.ds(pl.multiple_of(k * BACK, BACK), BACK)
        near = jnp.where(k < 16, b, other)
        flip = jnp.where(k < 16, other, b)
        return remote(
            wbuf.at[side, sl],
            returned.at[half, sl],
            s_ret.at[side, k],
            r_ret.at[half, k],
            (shifted(d, k, -1), near if side == 0 else flip),
        )

    def ret_wait(h, k):
        sl = pl.ds(pl.multiple_of(k * BACK, BACK), BACK)
        return remote(
            wbuf.at[0, sl],
            returned.at[h, sl],
            s_ret.at[0, k],
            r_ret.at[h, k],
            (shifted(d, k, 1), other),
        )

    stack2 = pile
    stack2[1120:1152, :] = stack_tail

    def send_back(side):
        def body(g, carry):
            for u in range(14):
                at = side * HALF + u * UNIT
                stack2[u * 80 : (u + 1) * 80, :] = rows[
                    pl.ds(pl.multiple_of(SLOTS + g * 80, 80), 80), at : at + UNIT
                ]
            wbuf[side, pl.ds(pl.multiple_of(g * 1152, 1152), 1152), :] = jnp.dot(
                perm_back[...], stack2[...], preferred_element_type=F32
            ).astype(BF)
            for i in range(8):
                k = g * 8 + i
                if side == 0:

                    @pl.when(k > 0)
                    def _():
                        ret_copy(0, k).start()
                else:
                    ret_copy(1, k).start()
            return carry

        lax.fori_loop(0, 4, body, 0)

    send_back(1)
    send_back(0)
    own_back = pltpu.make_async_copy(
        wbuf.at[0, pl.ds(0, BACK)], returned.at[half, pl.ds(0, BACK)], l_sem.at[3]
    )
    own_back.start()
    own_back.wait()

    def home(h):
        def body(g, carry):
            for i in range(8):
                k = g * 8 + i

                @pl.when(jnp.logical_or(k > 0, half != h))
                def _():
                    ret_wait(h, k).wait_recv()

            z = jnp.dot(
                perm_home[...],
                returned[h, pl.ds(pl.multiple_of(g * 1152, 1152), 1152), :],
                preferred_element_type=F32,
            ).astype(BF)
            for u in range(14):
                at = h * HALF + u * UNIT
                rows[pl.ds(pl.multiple_of(g * 80, 80), 80), at : at + UNIT] = z[
                    u * 80 : (u + 1) * 80, :
                ]
            return carry

        lax.fori_loop(0, 4, body, 0)

    home(0)
    home(1)
    for j in range(8):
        sl = slice(j * CHUNK, (j + 1) * CHUNK)
        both = jnp.dot(coef[...], rows[0:SLOTS, sl], preferred_element_type=F32)
        normed[:, sl] = (stream[:, sl] + both[0:TOK, :] + both[TOK : 2 * TOK, :]).astype(BF)
    result = pltpu.make_async_copy(normed, out, l_sem.at[4])
    result.start()

    for c in attn_out:
        c.wait_send()
    for a in range(3):
        first[a][0].wait_send()
        first[a][1].wait_send()
        second[a][0].wait_send()
        second[a][1].wait_send()
    for c in hid:
        c.wait_send()

    def drain(k, carry):
        @pl.when(k > 0)
        def _():
            disp_copy(k).wait_send()
            ret_copy(0, k).wait_send()

        fwd_copy(k).wait_send()
        ret_copy(1, k).wait_send()
        return carry

    lax.fori_loop(0, EXPERTS, drain, 0)
    result.wait()


def layer(attn, residual, gain, router, ids, pos, pos_t, gate, up, down):
    any_ = pl.BlockSpec(memory_space=pl.ANY)
    vmem = pl.BlockSpec(memory_space=pltpu.VMEM)
    dma = pltpu.SemaphoreType.DMA
    got = pl.pallas_call(
        kernel,
        out_shape=[
            jax.ShapeDtypeStruct((TOK, D), BF),
            jax.ShapeDtypeStruct((3, D, 128), BF),
            jax.ShapeDtypeStruct((3, D, 128), BF),
            jax.ShapeDtypeStruct((3, CHUNK, FF), BF),
        ],
        in_specs=[any_, any_, vmem, vmem, vmem, vmem, vmem, any_, any_, any_],
        out_specs=[any_] * 4,
        scratch_shapes=[
            pltpu.VMEM((32, TOK, PIECE), BF),
            pltpu.VMEM((TOK, D), F32),
            pltpu.VMEM((TOK, D), BF),
            pltpu.VMEM((640, 640), BF),
            pltpu.VMEM((1152, 1152), BF),
            pltpu.VMEM((1120, 1152), BF),
            pltpu.VMEM((640, CHUNK), BF),
            pltpu.VMEM((2560, CHUNK), BF),
            pltpu.VMEM((2, 2560, CHUNK), BF),
            pltpu.VMEM((2 * SLOTS, D), BF),
            pltpu.VMEM((2, D, UNIT), BF),
            pltpu.VMEM((2, CHUNK, FF), BF),
            pltpu.VMEM((2 * SLOTS, UNIT), F32),
            pltpu.VMEM((2, 2 * SLOTS, FF // 2), BF),
            pltpu.VMEM((1152, UNIT), BF),
            pltpu.VMEM((2, 32 * BACK, UNIT), BF),
            pltpu.VMEM((2 * TOK, SLOTS), BF),
            dma((32,)),
            dma((32,)),
            dma((3, 4)),
            dma((3, 4)),
            dma((32,)),
            dma((32,)),
            dma((32,)),
            dma((32,)),
            dma((2,)),
            dma((2,)),
            dma((2, 32)),
            dma((2, 32)),
            dma((5,)),
            dma((2, 3)),
        ],
        compiler_params=pltpu.CompilerParams(
            collective_id=0, has_side_effects=True, vmem_limit_bytes=64 * 1024 * 1024 - 4096
        ),
        cost_estimate=pl.CostEstimate(
            flops=20_000_000_000, bytes_accessed=80_000_000, transcendentals=400_000
        ),
    )(attn, residual, gain, router, ids, pos, pos_t, gate, up, down)
    return got[0]


def body(
    attn_cols, residual, norm_gain, router_weight, expert_ids, gate_weight, up_weight, down_weight
):
    d = lax.axis_index("dp")
    flat = expert_ids.reshape(-1)
    n = flat.shape[0]
    earlier = jnp.arange(n)[None, :] < jnp.arange(n)[:, None]
    rank = jnp.sum(
        jnp.logical_and(flat[:, None] == flat[None, :], earlier).astype(I32), axis=1
    ).reshape(expert_ids.shape)
    kx = (expert_ids // 16 - d // 16 + 2) % 2
    kz = ((expert_ids // 2) % 8 - (d // 2) % 8 + 8) % 8
    kc = (expert_ids % 2 - d % 2 + 2) % 2
    pos = (kx * 16 + kz * 2 + kc) * CAP + rank
    return layer(
        attn_cols,
        residual,
        norm_gain.reshape(1, D),
        router_weight,
        expert_ids,
        pos,
        pos.T,
        gate_weight,
        up_weight,
        down_weight,
    )


def solution(mesh):
    return jax.shard_map(
        body,
        mesh=mesh,
        in_specs=(
            P("blk", "dp"),
            P(("blk", "dp"), None),
            P(),
            P(),
            P(("blk", "dp"), None),
            P("dp", None, "blk"),
            P("dp", None, "blk"),
            P("dp", "blk", None),
        ),
        out_specs=P(("blk", "dp"), None),
        check_vma=False,
    )
```

```python
import jax
import jax.numpy as jnp
from jax import lax
from jax.experimental import pallas as pl
from jax.experimental.pallas import tpu as pltpu
from jax.sharding import PartitionSpec as P

BF = jnp.bfloat16
F32 = jnp.float32
I32 = jnp.int32
D = 7168
FF = 1024
TOK = 128
EXPERTS = 32
CAP = 10
SLOTS = EXPERTS * CAP
PIECE = 224
CHUNK = 896
HALF = D // 2
UNIT = 256
BACK = 144
MESH = pl.DeviceIdType.MESH


def div(a, n):
    return lax.div(a, jnp.int32(n))


def rem(a, n):
    return lax.rem(a, jnp.int32(n))


def shifted(d, k, sign):
    x = rem(div(d, 16) + k // 16, 2)
    z = rem(rem(div(d, 2), 8) + (sign * ((k // 2) % 8) + 8), 8)
    c = rem(rem(d, 2) + k % 2, 2)
    return x * 16 + z * 2 + c


def nt_dot(a, b):
    return lax.dot_general(a, b, (((1,), (1,)), ((), ())), preferred_element_type=F32)


def rows_at(start, n):
    return pl.ds(pl.multiple_of(start, 16), n)


def kernel(
    attn,
    residual,
    gain,
    router,
    ids,
    gate,
    up,
    down,
    out,
    gate_all,
    up_all,
    down_all,
    cols,
    stream,
    normed,
    gains,
    perm,
    perm_back,
    perm_home,
    stack,
    outgoing,
    arrived,
    rows,
    wbuf,
    dbuf,
    acc,
    hidden,
    pile,
    sending,
    returned,
    coef,
    s_attn,
    r_attn,
    s_ring,
    r_ring,
    s_disp,
    r_disp,
    s_fwd,
    r_fwd,
    s_hid,
    r_hid,
    s_ret,
    r_ret,
    l_sem,
    w_sem,
):
    d = lax.axis_index("dp")
    b = lax.axis_index("blk")
    other = rem(b + 4, 8)
    half = div(b, 4)
    far = 1 - half
    y = rem(b, 4)
    ring_r = half * 4 + rem(y + 1, 4)
    ring_l = half * 4 + rem(y + 3, 4)
    shard_of = (y, rem(y + 3, 4), rem(y + 1, 4), rem(y + 2, 4))

    def remote(src, dst, ss, rs, dev):
        return pltpu.make_async_remote_copy(
            src_ref=src,
            dst_ref=dst,
            send_sem=ss,
            recv_sem=rs,
            device_id=dev,
            device_id_type=MESH,
        )

    def lanes_at(start, n):
        return pl.ds(pl.multiple_of(start, 128), n)

    own_cols = pltpu.make_async_copy(
        attn.at[:, lanes_at(d * TOK, TOK)], cols.at[rows_at(d * PIECE, PIECE)], l_sem.at[0]
    )
    own_cols.start()
    own_res = pltpu.make_async_copy(residual, normed, l_sem.at[1])
    own_res.start()

    barrier = pltpu.get_barrier_semaphore()
    for k in range(EXPERTS):
        p = shifted(d, k, 1)
        for q in (b, other):
            if k == 0 and q is b:
                continue
            pl.semaphore_signal(barrier, inc=1, device_id=(p, q), device_id_type=MESH)
    for q in (ring_l, ring_r):
        pl.semaphore_signal(barrier, inc=1, device_id=(d, q), device_id_type=MESH)
    pl.semaphore_wait(barrier, 65)

    attn_out = []
    for k in range(1, 32):
        p = shifted(d, k, 1)
        c = remote(
            attn.at[:, lanes_at(p * TOK, TOK)],
            cols.at[rows_at(d * PIECE, PIECE)],
            s_attn.at[k],
            r_attn.at[k],
            (p, b),
        )
        c.start()
        attn_out.append(c)

    mine = (gate.at[0], up.at[0], down.at[0])
    gathered = (gate_all, up_all, down_all)
    first = {}
    second = {}

    def begin(a):
        c0 = remote(mine[a], gathered[a].at[0], s_ring.at[a, 0], r_ring.at[a, 0], (d, ring_r))
        c1 = remote(mine[a], gathered[a].at[1], s_ring.at[a, 1], r_ring.at[a, 1], (d, ring_l))
        c0.start()
        c1.start()
        first[a] = (c0, c1)

    def pass_on(a):
        n = gathered[a].shape[1] // 2
        c0, c1 = first[a]
        c0.wait_recv()
        f0 = remote(
            gathered[a].at[0, pl.ds(0, n)],
            gathered[a].at[2, pl.ds(0, n)],
            s_ring.at[a, 2],
            r_ring.at[a, 2],
            (d, ring_r),
        )
        f0.start()
        c1.wait_recv()
        f1 = remote(
            gathered[a].at[1, pl.ds(n, n)],
            gathered[a].at[2, pl.ds(n, n)],
            s_ring.at[a, 3],
            r_ring.at[a, 3],
            (d, ring_l),
        )
        f1.start()
        second[a] = (f0, f1)

    def complete(a):
        second[a][0].wait_recv()
        second[a][1].wait_recv()

    def fetch_in(slot):
        src = mine if slot == 0 else (gate_all.at[slot - 1], up_all.at[slot - 1])
        s = slot % 2
        cs = []
        for i in range(2):
            c = pltpu.make_async_copy(
                src[i], wbuf.at[s, :, pl.ds(i * 128, 128)], w_sem.at[s, i]
            )
            c.start()
            cs.append(c)
        return cs

    def fetch_out(slot):
        src = down.at[0] if slot == 0 else down_all.at[slot - 1]
        s = slot % 2
        c = pltpu.make_async_copy(src, dbuf.at[s], w_sem.at[s, 2])
        c.start()
        return c

    begin(0)
    begin(1)
    in_copies = {0: fetch_in(0)}
    out_copies = {0: fetch_out(0)}

    def fill(i, carry):
        at = rows_at(i * 16, 16)
        r = lax.broadcasted_iota(I32, (16, 128), 0) + i * 16
        lane = lax.broadcasted_iota(I32, (16, 128), 1)
        outer = lax.shift_right_logical(r * 14564, 21)
        inner = r - outer * BACK
        mid = lax.shift_right_logical(inner * 6554, 16)
        back = jnp.where(inner < 140, mid * 80 + outer * CAP + inner - mid * CAP, -1)
        outer = lax.shift_right_logical(r * 26215, 21)
        inner = r - outer * 80
        mid = lax.shift_right_logical(inner * 6554, 16)
        last = inner - mid * CAP
        home = mid * BACK + outer * CAP + last
        swap = mid * 80 + outer * CAP + last
        for j in range(9):
            sl = slice(j * 128, (j + 1) * 128)
            perm_back[at, sl] = jnp.where(lane + j * 128 == back, 1.0, 0.0).astype(BF)
            perm_home[at, sl] = jnp.where(lane + j * 128 == home, 1.0, 0.0).astype(BF)

        @pl.when(i < 40)
        def _():
            for j in range(5):
                sl = slice(j * 128, (j + 1) * 128)
                perm[at, sl] = jnp.where(lane + j * 128 == swap, 1.0, 0.0).astype(BF)

        return carry

    lax.fori_loop(0, 72, fill, 0)
    pile[1120:1152, :] = jnp.zeros((32, UNIT), BF)
    gains[...] = gain[...].astype(F32)

    names = lax.broadcasted_iota(I32, (EXPERTS, TOK), 0)
    named = [names == ids[m : m + 1, :] for m in range(2)]
    uses = jnp.where(jnp.logical_or(named[0], named[1]), 1.0, 0.0).astype(BF)
    t0 = lax.broadcasted_iota(I32, (TOK, TOK), 0)
    t1 = lax.broadcasted_iota(I32, (TOK, TOK), 1)
    eye = jnp.where(t0 == t1, 1.0, 0.0).astype(BF)
    earlier = jnp.dot(uses, jnp.where(t0 < t1, 1.0, 0.0).astype(BF), preferred_element_type=F32)
    ahead = (
        (div(names, 16) - div(d, 16) + 2) % 2 * 16
        + (rem(div(names, 2), 8) - rem(div(d, 2), 8) + 8) % 8 * 2
        + (rem(names, 2) - rem(d, 2) + 2) % 2
    )
    table = ahead.astype(F32) * CAP + earlier
    pos = [
        jnp.sum(jnp.where(named[m], table, 0.0), axis=0, keepdims=True).astype(I32)
        for m in range(2)
    ]

    for c in attn_out:
        c.wait_recv()
    own_cols.wait()
    own_res.wait()
    pass_on(0)

    def add_cols(i, total):
        at = lanes_at(i * UNIT, UNIT)
        s = normed[:, at].astype(F32) + nt_dot(eye, cols[rows_at(i * UNIT, UNIT), :])
        stream[:, at] = s
        sq = s * s
        return total + sq[:, 0:128] + sq[:, 128:256]

    total = lax.fori_loop(0, D // UNIT, add_cols, jnp.zeros((TOK, 128), F32))
    inv = lax.rsqrt(jnp.sum(total, axis=1, keepdims=True) * (1.0 / D) + 1e-06)

    def scale_cols(i, carry):
        at = lanes_at(i * 128, 128)
        normed[:, at] = (stream[:, at] * inv * gains[pl.ds(i, 1), :]).astype(BF)
        return carry

    lax.fori_loop(0, D // 128, scale_cols, 0)

    def disp_copy(k):
        at = rows_at(k * 80, 80)
        return remote(
            outgoing.at[at],
            arrived.at[0, at],
            s_disp.at[k],
            r_disp.at[k],
            (shifted(d, k, 1), jnp.where(k < 16, b, other)),
        )

    def dispatch(g, carry):
        want = lax.broadcasted_iota(I32, (80, TOK), 0) + g * 80
        hit = jnp.logical_or(want == pos[0], want == pos[1])
        one = jnp.where(hit, 1.0, 0.0).astype(BF)
        for j in range(8):
            stack[j * 80 : (j + 1) * 80, :] = jnp.dot(
                one, normed[:, j * CHUNK : (j + 1) * CHUNK], preferred_element_type=F32
            ).astype(BF)
        for n in range(0, CHUNK, UNIT):
            at = slice(n, min(n + UNIT, CHUNK))
            outgoing[rows_at(g * 640, 640), at] = jnp.dot(
                perm[...], stack[:, at], preferred_element_type=F32
            ).astype(BF)
        for i in range(8):
            k = g * 8 + i

            @pl.when(k > 0)
            def _():
                disp_copy(k).start()

        return carry

    lax.fori_loop(0, 4, dispatch, 0)
    own_rows = pltpu.make_async_copy(
        outgoing.at[pl.ds(0, 80)], arrived.at[0, pl.ds(0, 80)], l_sem.at[2]
    )
    own_rows.start()
    begin(2)

    logits = jnp.zeros((EXPERTS, TOK), F32)
    for q in range(8):
        sl = slice(q * CHUNK, (q + 1) * CHUNK)
        logits += nt_dot(router[:, sl], normed[:, sl])
    affinity = jax.nn.sigmoid(logits)
    chosen = [jnp.sum(jnp.where(n, affinity, 0.0), axis=0, keepdims=True) for n in named]
    scale = 2.5 / (chosen[0] + chosen[1])
    for part in range(2):
        where = lax.broadcasted_iota(I32, (160, TOK), 0) + part * 160
        full = jnp.where(where == pos[0], chosen[0] * scale, 0.0) + jnp.where(
            where == pos[1], chosen[1] * scale, 0.0
        )
        high = full.astype(BF)
        low = (full - high.astype(F32)).astype(BF)
        coef[part, 0:TOK, :] = nt_dot(eye, high).astype(BF)
        coef[part, TOK : 2 * TOK, :] = nt_dot(eye, low).astype(BF)

    def fwd_copy(k):
        at = rows_at(k * 80, 80)
        return remote(arrived.at[0, at], arrived.at[1, at], s_fwd.at[k], r_fwd.at[k], (d, other))

    def spread(side, g):
        base = div(g, 2) * SLOTS + side * 160 + rem(g, 2) * 80
        for n in range(0, CHUNK, UNIT):
            m = min(n + UNIT, CHUNK)
            z = jnp.dot(
                perm[...], arrived[side, rows_at(g * 640, 640), n:m], preferred_element_type=F32
            ).astype(BF)
            for j in range(8):
                rows[rows_at(base, 80), j * CHUNK + n : j * CHUNK + m] = z[j * 80 : (j + 1) * 80]

    def arrive(g, carry):
        for i in range(8):
            k = g * 8 + i

            @pl.when(k > 0)
            def _():
                disp_copy(k).wait_recv()

            fwd_copy(k).start()
        spread(0, g)
        return carry

    def arrive_other(g, carry):
        for i in range(8):
            fwd_copy(g * 8 + i).wait_recv()
        spread(1, g)
        return carry

    def project_in(batch):
        at = slice(batch * SLOTS, (batch + 1) * SLOTS)
        for slot in range(4):
            for c in in_copies[slot]:
                c.wait()

            def step(i, carry, slot=slot):
                ks = pl.ds(pl.multiple_of(i * 1024, 1024), 1024)
                part = jnp.dot(rows[at, ks], wbuf[slot % 2, ks, :], preferred_element_type=F32)

                @pl.when(i == 0)
                def _():
                    acc[...] = part

                @pl.when(i > 0)
                def _():
                    acc[...] += part

                return carry

            lax.fori_loop(0, 7, step, 0)
            g = acc[:, 0:128]
            h = (g / (1.0 + jnp.exp(-g)) * acc[:, 128:256]).astype(BF)
            hidden[0, at, lanes_at(shard_of[slot] * 128, 128)] = h
            nxt = slot + 2
            if nxt == 3 and batch == 0:
                complete(0)
                complete(1)
            if nxt < 4:
                in_copies[nxt] = fetch_in(nxt)
            elif batch == 0:
                in_copies[nxt - 4] = fetch_in(nxt - 4)
        cs = []
        for i in range(2):
            c = remote(
                hidden.at[0, pl.ds(batch * SLOTS + i * 160, 160)],
                hidden.at[1, pl.ds(batch * SLOTS + (1 - i) * 160, 160)],
                s_hid.at[batch, i],
                r_hid.at[batch, 1 - i],
                (d, other),
            )
            c.start()
            cs.append(c)
        return cs

    def project_out(batch):
        for slot in range(4):
            out_copies[slot].wait()
            at = slice(batch * SLOTS, (batch + 1) * SLOTS)
            for n in range(0, CHUNK, UNIT):
                w = min(UNIT, CHUNK - n)
                res = nt_dot(
                    hidden[0, at, :], dbuf[slot % 2, n : n + w, lanes_at(half * 512, 512)]
                )
                res += nt_dot(
                    hidden[1, at, :], dbuf[slot % 2, n : n + w, lanes_at(far * 512, 512)]
                )
                for side in range(2):
                    to = lanes_at(shard_of[slot] * CHUNK + side * HALF + n, w)
                    rows[batch * SLOTS : batch * SLOTS + 160, to] = res[
                        side * 160 : (side + 1) * 160
                    ].astype(BF)
            nxt = slot + 2
            if nxt < 4:
                if nxt == 3 and batch == 0:
                    complete(2)
                out_copies[nxt] = fetch_out(nxt)
            elif batch == 0:
                out_copies[nxt - 4] = fetch_out(nxt - 4)

    def ret_copy(side, k):
        at = rows_at(k * BACK, BACK)
        near = jnp.where(k < 16, b, other)
        flip = jnp.where(k < 16, other, b)
        return remote(
            sending.at[side, at],
            returned.at[half, at],
            s_ret.at[side, k],
            r_ret.at[half, k],
            (shifted(d, k, -1), near if side == 0 else flip),
        )

    def ret_wait(h, k):
        at = rows_at(k * BACK, BACK)
        return remote(
            sending.at[0, at],
            returned.at[h, at],
            s_ret.at[0, k],
            r_ret.at[h, k],
            (shifted(d, k, 1), other),
        )

    def send_back(batch):
        for side in (1, 0):

            def body(g, carry, side=side):
                base = batch * SLOTS + (g - batch * 2) * 80
                for u in range(14):
                    at = side * HALF + u * UNIT
                    pile[u * 80 : (u + 1) * 80, :] = rows[rows_at(base, 80), at : at + UNIT]
                sending[side, rows_at(g * 1152, 1152), :] = jnp.dot(
                    perm_back[...], pile[...], preferred_element_type=F32
                ).astype(BF)
                for i in range(8):
                    k = g * 8 + i
                    if side == 0 and batch == 0 and i == 0:

                        @pl.when(k > 0)
                        def _():
                            ret_copy(0, k).start()
                    else:
                        ret_copy(side, k).start()
                return carry

            lax.fori_loop(2 * batch, 2 * batch + 2, body, 0)

    def home(batch):
        for h in range(2):

            def body(g, carry, h=h):
                for i in range(8):
                    k = g * 8 + i
                    if batch == 0 and i == 0:

                        @pl.when(jnp.logical_or(k > 0, half != h))
                        def _():
                            ret_wait(h, k).wait_recv()
                    else:
                        ret_wait(h, k).wait_recv()
                z = jnp.dot(
                    perm_home[0:1120, :],
                    returned[h, rows_at(g * 1152, 1152), :],
                    preferred_element_type=F32,
                ).astype(BF)
                base = batch * SLOTS + 160 + (g - 2 * batch) * 80
                for u in range(14):
                    at = h * HALF + u * UNIT
                    rows[rows_at(base, 80), at : at + UNIT] = z[u * 80 : (u + 1) * 80, :]
                return carry

            lax.fori_loop(2 * batch, 2 * batch + 2, body, 0)

    def combine(batch):
        def body(i, carry):
            at = lanes_at(i * 512, 512)
            both = jnp.dot(
                coef[batch],
                rows[batch * SLOTS + 160 : (batch + 1) * SLOTS, at],
                preferred_element_type=F32,
            )
            s = stream[:, at] + both[0:TOK, :] + both[TOK : 2 * TOK, :]
            if batch == 0:
                stream[:, at] = s
            else:
                normed[:, at] = s.astype(BF)
            return carry

        lax.fori_loop(0, D // 512, body, 0)

    own_rows.wait()
    lax.fori_loop(0, 1, arrive, 0)
    pass_on(1)
    in_copies[1] = fetch_in(1)
    lax.fori_loop(1, 2, arrive, 0)
    lax.fori_loop(0, 2, arrive_other, 0)
    pass_on(2)
    out_copies[1] = fetch_out(1)
    hid_a = project_in(0)
    lax.fori_loop(2, 3, arrive, 0)
    for c in hid_a:
        c.wait_recv()
    project_out(0)
    send_back(0)
    own_back = pltpu.make_async_copy(
        sending.at[0, pl.ds(0, BACK)], returned.at[half, pl.ds(0, BACK)], l_sem.at[3]
    )
    own_back.start()
    lax.fori_loop(3, 4, arrive, 0)
    lax.fori_loop(2, 4, arrive_other, 0)
    hid_b = project_in(1)
    for c in hid_b:
        c.wait_recv()
    project_out(1)
    send_back(1)
    own_back.wait()
    home(0)
    combine(0)
    home(1)
    combine(1)
    result = pltpu.make_async_copy(normed, out, l_sem.at[4])
    result.start()

    for c in attn_out:
        c.wait_send()
    for a in range(3):
        for c in first[a] + second[a]:
            c.wait_send()
    for c in hid_a + hid_b:
        c.wait_send()

    def drain(k, carry):
        @pl.when(k > 0)
        def _():
            disp_copy(k).wait_send()
            ret_copy(0, k).wait_send()

        fwd_copy(k).wait_send()
        ret_copy(1, k).wait_send()
        return carry

    lax.fori_loop(0, EXPERTS, drain, 0)
    result.wait()


def layer(attn, residual, gain, router, ids, gate, up, down):
    any_ = pl.BlockSpec(memory_space=pl.ANY)
    vmem = pl.BlockSpec(memory_space=pltpu.VMEM)
    dma = pltpu.SemaphoreType.DMA
    got = pl.pallas_call(
        kernel,
        out_shape=[
            jax.ShapeDtypeStruct((TOK, D), BF),
            jax.ShapeDtypeStruct((3, D, 128), BF),
            jax.ShapeDtypeStruct((3, D, 128), BF),
            jax.ShapeDtypeStruct((3, CHUNK, FF), BF),
        ],
        in_specs=[any_, any_, vmem, vmem, vmem, any_, any_, any_],
        out_specs=[any_] * 4,
        scratch_shapes=[
            pltpu.VMEM((D, TOK), BF),
            pltpu.VMEM((TOK, D), F32),
            pltpu.VMEM((TOK, D), BF),
            pltpu.VMEM((56, 128), F32),
            pltpu.VMEM((640, 640), BF),
            pltpu.VMEM((1152, 1152), BF),
            pltpu.VMEM((1152, 1152), BF),
            pltpu.VMEM((640, CHUNK), BF),
            pltpu.VMEM((2560, CHUNK), BF),
            pltpu.VMEM((2, 2560, CHUNK), BF),
            pltpu.VMEM((2 * SLOTS, D), BF),
            pltpu.VMEM((2, D, UNIT), BF),
            pltpu.VMEM((2, CHUNK, FF), BF),
            pltpu.VMEM((SLOTS, UNIT), F32),
            pltpu.VMEM((2, 2 * SLOTS, FF // 2), BF),
            pltpu.VMEM((1152, UNIT), BF),
            pltpu.VMEM((2, 32 * BACK, UNIT), BF),
            pltpu.VMEM((2, 32 * BACK, UNIT), BF),
            pltpu.VMEM((2, 2 * TOK, 160), BF),
            dma((32,)),
            dma((32,)),
            dma((3, 4)),
            dma((3, 4)),
            dma((32,)),
            dma((32,)),
            dma((32,)),
            dma((32,)),
            dma((2, 2)),
            dma((2, 2)),
            dma((2, 32)),
            dma((2, 32)),
            dma((5,)),
            dma((2, 3)),
        ],
        compiler_params=pltpu.CompilerParams(
            collective_id=0, has_side_effects=True, vmem_limit_bytes=64 * 1024 * 1024 - 4096
        ),
        cost_estimate=pl.CostEstimate(
            flops=20_000_000_000, bytes_accessed=80_000_000, transcendentals=400_000
        ),
    )(attn, residual, gain, router, ids, gate, up, down)
    return got[0]


def body(
    attn_cols, residual, norm_gain, router_weight, expert_ids, gate_weight, up_weight, down_weight
):
    return layer(
        attn_cols.T,
        residual,
        norm_gain.reshape(D // 128, 128),
        router_weight.T,
        expert_ids.T,
        gate_weight,
        up_weight,
        down_weight,
    )


def solution(mesh):
    return jax.shard_map(
        body,
        mesh=mesh,
        in_specs=(
            P("blk", "dp"),
            P(("blk", "dp"), None),
            P(),
            P(),
            P(("blk", "dp"), None),
            P("dp", None, "blk"),
            P("dp", None, "blk"),
            P("dp", "blk", None),
        ),
        out_specs=P(("blk", "dp"), None),
        check_vma=False,
    )
```

```python
import jax
import jax.numpy as jnp
from jax import lax
from jax.experimental import pallas as pl
from jax.experimental.pallas import tpu as pltpu
from jax.sharding import PartitionSpec as P

BF = jnp.bfloat16
F32 = jnp.float32
I32 = jnp.int32
D = 7168
FF = 1024
TOK = 128
EXPERTS = 32
CAP = 10
SLOTS = EXPERTS * CAP
PIECE = 224
CHUNK = 896
HALF = D // 2
UNIT = 256
BACK = 144
MESH = pl.DeviceIdType.MESH


def div(a, n):
    return lax.div(a, jnp.int32(n))


def rem(a, n):
    return lax.rem(a, jnp.int32(n))


def shifted(d, k, sign):
    x = rem(div(d, 16) + k // 16, 2)
    i = (k // 2) % 8
    step = (i % 2) * ((i + 1) // 2) + (1 - i % 2) * ((8 - i // 2) % 8)
    z = rem(rem(div(d, 2), 8) + (sign * step + 8), 8)
    c = rem(rem(d, 2) + k % 2, 2)
    return x * 16 + z * 2 + c


def nt_dot(a, b):
    return lax.dot_general(a, b, (((1,), (1,)), ((), ())), preferred_element_type=F32)


def rows_at(start, n):
    return pl.ds(pl.multiple_of(start, 16), n)


def kernel(
    attn,
    residual,
    gain,
    router,
    ids,
    gate,
    up,
    down,
    out,
    gate_all,
    up_all,
    down_all,
    cols,
    stream,
    normed,
    gains,
    perm,
    perm_back,
    perm_home,
    stack,
    outgoing,
    arrived,
    rows,
    wbuf,
    dbuf,
    acc,
    hidden,
    pile,
    sending,
    returned,
    coef,
    s_attn,
    r_attn,
    s_ring,
    r_ring,
    s_disp,
    r_disp,
    s_fwd,
    r_fwd,
    s_hid,
    r_hid,
    s_ret,
    r_ret,
    l_sem,
    w_sem,
):
    d = lax.axis_index("dp")
    b = lax.axis_index("blk")
    other = rem(b + 4, 8)
    half = div(b, 4)
    far = 1 - half
    y = rem(b, 4)
    ring_r = half * 4 + rem(y + 1, 4)
    ring_l = half * 4 + rem(y + 3, 4)
    shard_of = (y, rem(y + 3, 4), rem(y + 1, 4), rem(y + 2, 4))

    def remote(src, dst, ss, rs, dev):
        return pltpu.make_async_remote_copy(
            src_ref=src,
            dst_ref=dst,
            send_sem=ss,
            recv_sem=rs,
            device_id=dev,
            device_id_type=MESH,
        )

    def lanes_at(start, n):
        return pl.ds(pl.multiple_of(start, 128), n)

    own_cols = pltpu.make_async_copy(
        attn.at[:, lanes_at(d * TOK, TOK)], cols.at[rows_at(d * PIECE, PIECE)], l_sem.at[0]
    )
    own_cols.start()
    own_res = pltpu.make_async_copy(residual, normed, l_sem.at[1])
    own_res.start()

    barrier = pltpu.get_barrier_semaphore()
    for k in range(EXPERTS):
        p = shifted(d, k, 1)
        for q in (b, other):
            if k == 0 and q is b:
                continue
            pl.semaphore_signal(barrier, inc=1, device_id=(p, q), device_id_type=MESH)
    for q in (ring_l, ring_r):
        pl.semaphore_signal(barrier, inc=1, device_id=(d, q), device_id_type=MESH)
    pl.semaphore_wait(barrier, 65)

    attn_out = []
    for k in range(1, 32):
        p = shifted(d, k, 1)
        c = remote(
            attn.at[:, lanes_at(p * TOK, TOK)],
            cols.at[rows_at(d * PIECE, PIECE)],
            s_attn.at[k],
            r_attn.at[k],
            (p, b),
        )
        c.start()
        attn_out.append(c)

    mine = (gate.at[0], up.at[0], down.at[0])
    gathered = (gate_all, up_all, down_all)
    first = {}
    second = {}

    def begin(a):
        c0 = remote(mine[a], gathered[a].at[0], s_ring.at[a, 0], r_ring.at[a, 0], (d, ring_r))
        c1 = remote(mine[a], gathered[a].at[1], s_ring.at[a, 1], r_ring.at[a, 1], (d, ring_l))
        c0.start()
        c1.start()
        first[a] = (c0, c1)

    def pass_on(a):
        n = gathered[a].shape[1] // 2
        c0, c1 = first[a]
        c0.wait_recv()
        f0 = remote(
            gathered[a].at[0, pl.ds(0, n)],
            gathered[a].at[2, pl.ds(0, n)],
            s_ring.at[a, 2],
            r_ring.at[a, 2],
            (d, ring_r),
        )
        f0.start()
        c1.wait_recv()
        f1 = remote(
            gathered[a].at[1, pl.ds(n, n)],
            gathered[a].at[2, pl.ds(n, n)],
            s_ring.at[a, 3],
            r_ring.at[a, 3],
            (d, ring_l),
        )
        f1.start()
        second[a] = (f0, f1)

    def complete(a):
        second[a][0].wait_recv()
        second[a][1].wait_recv()

    def fetch_in(slot):
        src = mine if slot == 0 else (gate_all.at[slot - 1], up_all.at[slot - 1])
        s = slot % 2
        cs = []
        for i in range(2):
            c = pltpu.make_async_copy(
                src[i], wbuf.at[s, :, pl.ds(i * 128, 128)], w_sem.at[s, i]
            )
            c.start()
            cs.append(c)
        return cs

    def fetch_out(slot):
        src = down.at[0] if slot == 0 else down_all.at[slot - 1]
        s = slot % 2
        c = pltpu.make_async_copy(src, dbuf.at[s], w_sem.at[s, 2])
        c.start()
        return c

    for a in range(3):
        begin(a)
    in_copies = {0: fetch_in(0)}
    out_copies = {0: fetch_out(0)}

    def fill(i, carry):
        at = rows_at(i * 16, 16)
        r = lax.broadcasted_iota(I32, (16, 128), 0) + i * 16
        lane = lax.broadcasted_iota(I32, (16, 128), 1)
        outer = lax.shift_right_logical(r * 14564, 21)
        inner = r - outer * BACK
        mid = lax.shift_right_logical(inner * 6554, 16)
        back = jnp.where(inner < 140, mid * 80 + outer * CAP + inner - mid * CAP, -1)
        outer = lax.shift_right_logical(r * 26215, 21)
        inner = r - outer * 80
        mid = lax.shift_right_logical(inner * 6554, 16)
        last = inner - mid * CAP
        home = mid * BACK + outer * CAP + last
        swap = mid * 80 + outer * CAP + last
        for j in range(9):
            sl = slice(j * 128, (j + 1) * 128)
            perm_back[at, sl] = jnp.where(lane + j * 128 == back, 1.0, 0.0).astype(BF)
            perm_home[at, sl] = jnp.where(lane + j * 128 == home, 1.0, 0.0).astype(BF)

        @pl.when(i < 40)
        def _():
            for j in range(5):
                sl = slice(j * 128, (j + 1) * 128)
                perm[at, sl] = jnp.where(lane + j * 128 == swap, 1.0, 0.0).astype(BF)

        return carry

    lax.fori_loop(0, 72, fill, 0)
    pile[1120:1152, :] = jnp.zeros((32, UNIT), BF)
    gains[...] = gain[...].astype(F32)

    names = lax.broadcasted_iota(I32, (EXPERTS, TOK), 0)
    named = [names == ids[m : m + 1, :] for m in range(2)]
    uses = jnp.where(jnp.logical_or(named[0], named[1]), 1.0, 0.0).astype(BF)
    t0 = lax.broadcasted_iota(I32, (TOK, TOK), 0)
    t1 = lax.broadcasted_iota(I32, (TOK, TOK), 1)
    eye = jnp.where(t0 == t1, 1.0, 0.0).astype(BF)
    earlier = jnp.dot(uses, jnp.where(t0 < t1, 1.0, 0.0).astype(BF), preferred_element_type=F32)
    step = (rem(div(names, 2), 8) - rem(div(d, 2), 8) + 8) % 8
    order = jnp.where(step > 4, 16 - 2 * step, jnp.maximum(2 * step - 1, 0))
    ahead = (
        (div(names, 16) - div(d, 16) + 2) % 2 * 16
        + order * 2
        + (rem(names, 2) - rem(d, 2) + 2) % 2
    )
    table = ahead.astype(F32) * CAP + earlier
    pos = [
        jnp.sum(jnp.where(named[m], table, 0.0), axis=0, keepdims=True).astype(I32)
        for m in range(2)
    ]

    for c in attn_out:
        c.wait_recv()
    own_cols.wait()
    own_res.wait()
    pass_on(0)

    def add_cols(i, total):
        at = lanes_at(i * UNIT, UNIT)
        s = normed[:, at].astype(F32) + nt_dot(eye, cols[rows_at(i * UNIT, UNIT), :])
        stream[:, at] = s
        sq = s * s
        return total + sq[:, 0:128] + sq[:, 128:256]

    total = lax.fori_loop(0, D // UNIT, add_cols, jnp.zeros((TOK, 128), F32))
    inv = lax.rsqrt(jnp.sum(total, axis=1, keepdims=True) * (1.0 / D) + 1e-06)

    def scale_cols(i, carry):
        at = lanes_at(i * 128, 128)
        normed[:, at] = (stream[:, at] * inv * gains[pl.ds(i, 1), :]).astype(BF)
        return carry

    lax.fori_loop(0, D // 128, scale_cols, 0)

    def disp_copy(k):
        at = rows_at(k * 80, 80)
        return remote(
            outgoing.at[at],
            arrived.at[0, at],
            s_disp.at[k],
            r_disp.at[k],
            (shifted(d, k, 1), jnp.where(jnp.int32(k) < 16, b, other)),
        )

    def dispatch(g, carry):
        want = lax.broadcasted_iota(I32, (80, TOK), 0) + g * 80
        hit = jnp.logical_or(want == pos[0], want == pos[1])
        one = jnp.where(hit, 1.0, 0.0).astype(BF)
        for j in range(8):
            stack[j * 80 : (j + 1) * 80, :] = jnp.dot(
                one, normed[:, j * CHUNK : (j + 1) * CHUNK], preferred_element_type=F32
            ).astype(BF)
        for n in range(0, CHUNK, UNIT):
            at = slice(n, min(n + UNIT, CHUNK))
            outgoing[rows_at(g * 640, 640), at] = jnp.dot(
                perm[...], stack[:, at], preferred_element_type=F32
            ).astype(BF)
        for i in range(8):
            k = g * 8 + i

            @pl.when(k > 0)
            def _():
                disp_copy(k).start()

        return carry

    lax.fori_loop(0, 4, dispatch, 0)
    own_rows = pltpu.make_async_copy(
        outgoing.at[pl.ds(0, 80)], arrived.at[0, pl.ds(0, 80)], l_sem.at[2]
    )
    own_rows.start()

    logits = jnp.zeros((EXPERTS, TOK), F32)
    for q in range(8):
        sl = slice(q * CHUNK, (q + 1) * CHUNK)
        logits += nt_dot(router[:, sl], normed[:, sl])
    affinity = jax.nn.sigmoid(logits)
    chosen = [jnp.sum(jnp.where(n, affinity, 0.0), axis=0, keepdims=True) for n in named]
    scale = 2.5 / (chosen[0] + chosen[1])
    for part in range(2):
        where = lax.broadcasted_iota(I32, (160, TOK), 0) + part * 160
        full = jnp.where(where == pos[0], chosen[0] * scale, 0.0) + jnp.where(
            where == pos[1], chosen[1] * scale, 0.0
        )
        high = full.astype(BF)
        low = (full - high.astype(F32)).astype(BF)
        coef[part, 0:TOK, :] = nt_dot(eye, high).astype(BF)
        coef[part, TOK : 2 * TOK, :] = nt_dot(eye, low).astype(BF)

    def fwd_copy(k):
        at = rows_at(k * 80, 80)
        return remote(arrived.at[0, at], arrived.at[1, at], s_fwd.at[k], r_fwd.at[k], (d, other))

    def spread(side, g):
        base = (g // 2) * SLOTS + side * 160 + (g % 2) * 80
        for n in range(0, CHUNK, UNIT):
            m = min(n + UNIT, CHUNK)
            z = jnp.dot(
                perm[...], arrived[side, rows_at(g * 640, 640), n:m], preferred_element_type=F32
            ).astype(BF)
            for j in range(8):
                rows[rows_at(base, 80), j * CHUNK + n : j * CHUNK + m] = z[j * 80 : (j + 1) * 80]

    def take(first_k, n):
        for k in range(first_k, first_k + n):
            if k > 0:
                disp_copy(k).wait_recv()
            fwd_copy(k).start()

    def arrive_other(g, carry):
        for i in range(8):
            fwd_copy(g * 8 + i).wait_recv()
        spread(1, g)
        return carry

    def project_in(batch, slot):
        at = slice(batch * SLOTS, (batch + 1) * SLOTS)
        for c in in_copies[slot]:
            c.wait()

        def step(i, carry):
            ks = pl.ds(pl.multiple_of(i * 1024, 1024), 1024)
            part = jnp.dot(rows[at, ks], wbuf[slot % 2, ks, :], preferred_element_type=F32)

            @pl.when(i == 0)
            def _():
                acc[...] = part

            @pl.when(i > 0)
            def _():
                acc[...] += part

            return carry

        lax.fori_loop(0, 7, step, 0)
        g = acc[:, 0:128]
        h = (g / (1.0 + jnp.exp(-g)) * acc[:, 128:256]).astype(BF)
        hidden[0, at, lanes_at(shard_of[slot] * 128, 128)] = h

    def swap_hidden(batch):
        cs = []
        for i in range(2):
            c = remote(
                hidden.at[0, pl.ds(batch * SLOTS + i * 160, 160)],
                hidden.at[1, pl.ds(batch * SLOTS + (1 - i) * 160, 160)],
                s_hid.at[batch, i],
                r_hid.at[batch, 1 - i],
                (d, other),
            )
            c.start()
            cs.append(c)
        return cs

    def project_out(batch):
        for slot in range(4):
            out_copies[slot].wait()
            at = slice(batch * SLOTS, (batch + 1) * SLOTS)
            for n in range(0, CHUNK, UNIT):
                w = min(UNIT, CHUNK - n)
                res = nt_dot(
                    hidden[0, at, :], dbuf[slot % 2, n : n + w, lanes_at(half * 512, 512)]
                )
                res += nt_dot(
                    hidden[1, at, :], dbuf[slot % 2, n : n + w, lanes_at(far * 512, 512)]
                )
                for side in range(2):
                    to = lanes_at(shard_of[slot] * CHUNK + side * HALF + n, w)
                    rows[batch * SLOTS : batch * SLOTS + 160, to] = res[
                        side * 160 : (side + 1) * 160
                    ].astype(BF)
            if slot == 0:
                out_copies[2] = fetch_out(2)
            elif slot == 2 and batch == 0:
                complete(2)
                out_copies[3] = fetch_out(3)
                out_copies[0] = fetch_out(0)
            elif slot == 1 and batch == 1:
                out_copies[3] = fetch_out(3)
            elif slot == 3 and batch == 0:
                out_copies[1] = fetch_out(1)

    def ret_copy(side, k):
        at = rows_at(k * BACK, BACK)
        near = jnp.where(k < 16, b, other)
        flip = jnp.where(k < 16, other, b)
        return remote(
            sending.at[side, at],
            returned.at[half, at],
            s_ret.at[side, k],
            r_ret.at[half, k],
            (shifted(d, k, -1), near if side == 0 else flip),
        )

    def ret_wait(h, k):
        at = rows_at(k * BACK, BACK)
        return remote(
            sending.at[0, at],
            returned.at[h, at],
            s_ret.at[0, k],
            r_ret.at[h, k],
            (shifted(d, k, 1), other),
        )

    def send_back(batch):
        for side in (1, 0):

            def body(g, carry, side=side):
                base = batch * SLOTS + (g - batch * 2) * 80
                for u in range(14):
                    at = side * HALF + u * UNIT
                    pile[u * 80 : (u + 1) * 80, :] = rows[rows_at(base, 80), at : at + UNIT]
                sending[side, rows_at(g * 1152, 1152), :] = jnp.dot(
                    perm_back[...], pile[...], preferred_element_type=F32
                ).astype(BF)
                for i in range(8):
                    k = g * 8 + i
                    if side == 0 and batch == 0 and i == 0:

                        @pl.when(k > 0)
                        def _():
                            ret_copy(0, k).start()
                    else:
                        ret_copy(side, k).start()
                return carry

            lax.fori_loop(2 * batch, 2 * batch + 2, body, 0)

    def home(batch):
        for h in range(2):

            def body(g, carry, h=h):
                for i in range(8):
                    k = g * 8 + i
                    if batch == 0 and i == 0:

                        @pl.when(jnp.logical_or(k > 0, half != h))
                        def _():
                            ret_wait(h, k).wait_recv()
                    else:
                        ret_wait(h, k).wait_recv()
                z = jnp.dot(
                    perm_home[0:1120, :],
                    returned[h, rows_at(g * 1152, 1152), :],
                    preferred_element_type=F32,
                ).astype(BF)
                base = batch * SLOTS + 160 + (g - 2 * batch) * 80
                for u in range(14):
                    at = h * HALF + u * UNIT
                    rows[rows_at(base, 80), at : at + UNIT] = z[u * 80 : (u + 1) * 80, :]
                return carry

            lax.fori_loop(2 * batch, 2 * batch + 2, body, 0)

    def combine(batch):
        def body(i, carry):
            at = lanes_at(i * 512, 512)
            both = jnp.dot(
                coef[batch],
                rows[batch * SLOTS + 160 : (batch + 1) * SLOTS, at],
                preferred_element_type=F32,
            )
            s = stream[:, at] + both[0:TOK, :] + both[TOK : 2 * TOK, :]
            if batch == 0:
                stream[:, at] = s
            else:
                normed[:, at] = s.astype(BF)
            return carry

        lax.fori_loop(0, D // 512, body, 0)

    own_rows.wait()
    take(0, 8)
    pass_on(1)
    in_copies[1] = fetch_in(1)
    spread(0, 0)
    take(8, 8)
    spread(0, 1)
    lax.fori_loop(0, 2, arrive_other, 0)
    pass_on(2)
    out_copies[1] = fetch_out(1)
    take(16, 4)
    project_in(0, 0)
    in_copies[2] = fetch_in(2)
    project_in(0, 1)
    project_in(0, 2)
    in_copies[0] = fetch_in(0)
    take(20, 4)
    complete(0)
    complete(1)
    in_copies[3] = fetch_in(3)
    spread(0, 2)
    project_in(0, 3)
    in_copies[1] = fetch_in(1)
    hid_a = swap_hidden(0)
    take(24, 4)
    for c in hid_a:
        c.wait_recv()
    project_out(0)
    send_back(0)
    own_back = pltpu.make_async_copy(
        sending.at[0, pl.ds(0, BACK)], returned.at[half, pl.ds(0, BACK)], l_sem.at[3]
    )
    own_back.start()
    take(28, 4)
    spread(0, 3)
    lax.fori_loop(2, 4, arrive_other, 0)
    project_in(1, 0)
    in_copies[2] = fetch_in(2)
    project_in(1, 1)
    in_copies[3] = fetch_in(3)
    project_in(1, 2)
    project_in(1, 3)
    hid_b = swap_hidden(1)
    for c in hid_b:
        c.wait_recv()
    project_out(1)
    send_back(1)
    own_back.wait()
    home(0)
    combine(0)
    home(1)
    combine(1)
    result = pltpu.make_async_copy(normed, out, l_sem.at[4])
    result.start()

    for c in attn_out:
        c.wait_send()
    for a in range(3):
        for c in first[a] + second[a]:
            c.wait_send()
    for c in hid_a + hid_b:
        c.wait_send()

    def drain(k, carry):
        @pl.when(k > 0)
        def _():
            disp_copy(k).wait_send()
            ret_copy(0, k).wait_send()

        fwd_copy(k).wait_send()
        ret_copy(1, k).wait_send()
        return carry

    lax.fori_loop(0, EXPERTS, drain, 0)
    result.wait()


def layer(attn, residual, gain, router, ids, gate, up, down):
    any_ = pl.BlockSpec(memory_space=pl.ANY)
    vmem = pl.BlockSpec(memory_space=pltpu.VMEM)
    dma = pltpu.SemaphoreType.DMA
    got = pl.pallas_call(
        kernel,
        out_shape=[
            jax.ShapeDtypeStruct((TOK, D), BF),
            jax.ShapeDtypeStruct((3, D, 128), BF),
            jax.ShapeDtypeStruct((3, D, 128), BF),
            jax.ShapeDtypeStruct((3, CHUNK, FF), BF),
        ],
        in_specs=[any_, any_, vmem, vmem, vmem, any_, any_, any_],
        out_specs=[any_] * 4,
        scratch_shapes=[
            pltpu.VMEM((D, TOK), BF),
            pltpu.VMEM((TOK, D), F32),
            pltpu.VMEM((TOK, D), BF),
            pltpu.VMEM((56, 128), F32),
            pltpu.VMEM((640, 640), BF),
            pltpu.VMEM((1152, 1152), BF),
            pltpu.VMEM((1152, 1152), BF),
            pltpu.VMEM((640, CHUNK), BF),
            pltpu.VMEM((2560, CHUNK), BF),
            pltpu.VMEM((2, 2560, CHUNK), BF),
            pltpu.VMEM((2 * SLOTS, D), BF),
            pltpu.VMEM((2, D, UNIT), BF),
            pltpu.VMEM((2, CHUNK, FF), BF),
            pltpu.VMEM((SLOTS, UNIT), F32),
            pltpu.VMEM((2, 2 * SLOTS, FF // 2), BF),
            pltpu.VMEM((1152, UNIT), BF),
            pltpu.VMEM((2, 32 * BACK, UNIT), BF),
            pltpu.VMEM((2, 32 * BACK, UNIT), BF),
            pltpu.VMEM((2, 2 * TOK, 160), BF),
            dma((32,)),
            dma((32,)),
            dma((3, 4)),
            dma((3, 4)),
            dma((32,)),
            dma((32,)),
            dma((32,)),
            dma((32,)),
            dma((2, 2)),
            dma((2, 2)),
            dma((2, 32)),
            dma((2, 32)),
            dma((5,)),
            dma((2, 3)),
        ],
        compiler_params=pltpu.CompilerParams(
            collective_id=0, has_side_effects=True, vmem_limit_bytes=64 * 1024 * 1024 - 4096
        ),
        cost_estimate=pl.CostEstimate(
            flops=20_000_000_000, bytes_accessed=80_000_000, transcendentals=400_000
        ),
    )(attn, residual, gain, router, ids, gate, up, down)
    return got[0]


def body(
    attn_cols, residual, norm_gain, router_weight, expert_ids, gate_weight, up_weight, down_weight
):
    return layer(
        attn_cols.T,
        residual,
        norm_gain.reshape(D // 128, 128),
        router_weight.T,
        expert_ids.T,
        gate_weight,
        up_weight,
        down_weight,
    )


def solution(mesh):
    return jax.shard_map(
        body,
        mesh=mesh,
        in_specs=(
            P("blk", "dp"),
            P(("blk", "dp"), None),
            P(),
            P(),
            P(("blk", "dp"), None),
            P("dp", None, "blk"),
            P("dp", None, "blk"),
            P("dp", "blk", None),
        ),
        out_specs=P(("blk", "dp"), None),
        check_vma=False,
    )
```

```python
import jax
import jax.numpy as jnp
from jax import lax
from jax.experimental import pallas as pl
from jax.experimental.pallas import tpu as pltpu
from jax.sharding import PartitionSpec as P

BF = jnp.bfloat16
F32 = jnp.float32
I32 = jnp.int32
D = 7168
FF = 1024
TOK = 128
EXPERTS = 32
CAP = 10
SLOTS = EXPERTS * CAP
PIECE = 224
CHUNK = 896
HALF = D // 2
UNIT = 256
BACK = 144
AHEAD = 7
MESH = pl.DeviceIdType.MESH


def div(a, n):
    return lax.div(a, jnp.int32(n))


def rem(a, n):
    return lax.rem(a, jnp.int32(n))


def shifted(d, k, sign):
    x = rem(div(d, 16) + k // 16, 2)
    i = (k // 2) % 8
    step = (i % 2) * ((i + 1) // 2) + (1 - i % 2) * ((8 - i // 2) % 8)
    z = rem(rem(div(d, 2), 8) + (sign * step + 8), 8)
    c = rem(rem(d, 2) + k % 2, 2)
    return x * 16 + z * 2 + c


def nt_dot(a, b):
    return lax.dot_general(a, b, (((1,), (1,)), ((), ())), preferred_element_type=F32)


def rows_at(start, n):
    return pl.ds(pl.multiple_of(start, 16), n)


def kernel(
    attn,
    residual,
    gain,
    router,
    ids,
    gate,
    up,
    down,
    out,
    gate_all,
    up_all,
    down_all,
    cols,
    stream,
    normed,
    gains,
    perm,
    perm_back,
    perm_home,
    stack,
    outgoing,
    arrived,
    rows,
    wbuf,
    dbuf,
    acc,
    hidden,
    pile,
    sending,
    returned,
    coef,
    s_attn,
    r_attn,
    s_ring,
    r_ring,
    s_disp,
    r_disp,
    s_fwd,
    r_fwd,
    s_hid,
    r_hid,
    s_ret,
    r_ret,
    l_sem,
    w_sem,
):
    d = lax.axis_index("dp")
    b = lax.axis_index("blk")
    other = rem(b + 4, 8)
    half = div(b, 4)
    far = 1 - half
    y = rem(b, 4)
    ring_r = half * 4 + rem(y + 1, 4)
    ring_l = half * 4 + rem(y + 3, 4)
    shard_of = (y, rem(y + 3, 4), rem(y + 1, 4), rem(y + 2, 4))

    def remote(src, dst, ss, rs, dev):
        return pltpu.make_async_remote_copy(
            src_ref=src,
            dst_ref=dst,
            send_sem=ss,
            recv_sem=rs,
            device_id=dev,
            device_id_type=MESH,
        )

    def lanes_at(start, n):
        return pl.ds(pl.multiple_of(start, 128), n)

    own_cols = pltpu.make_async_copy(
        attn.at[:, lanes_at(d * TOK, TOK)], cols.at[rows_at(d * PIECE, PIECE)], l_sem.at[0]
    )
    own_cols.start()
    own_res = pltpu.make_async_copy(residual, normed, l_sem.at[1])
    own_res.start()

    barrier = pltpu.get_barrier_semaphore()
    for k in range(EXPERTS):
        p = shifted(d, k, 1)
        for q in (b, other):
            if k == 0 and q is b:
                continue
            pl.semaphore_signal(barrier, inc=1, device_id=(p, q), device_id_type=MESH)
    for q in (ring_l, ring_r):
        pl.semaphore_signal(barrier, inc=1, device_id=(d, q), device_id_type=MESH)
    pl.semaphore_wait(barrier, 65)

    attn_out = []
    for k in range(1, 32):
        p = shifted(d, k, 1)
        c = remote(
            attn.at[:, lanes_at(p * TOK, TOK)],
            cols.at[rows_at(d * PIECE, PIECE)],
            s_attn.at[k],
            r_attn.at[k],
            (p, b),
        )
        c.start()
        attn_out.append(c)

    mine = (gate.at[0], up.at[0], down.at[0])
    gathered = (gate_all, up_all, down_all)
    first = {}
    second = {}

    def begin(a):
        c0 = remote(mine[a], gathered[a].at[0], s_ring.at[a, 0], r_ring.at[a, 0], (d, ring_r))
        c1 = remote(mine[a], gathered[a].at[1], s_ring.at[a, 1], r_ring.at[a, 1], (d, ring_l))
        c0.start()
        c1.start()
        first[a] = (c0, c1)

    def pass_on(a):
        n = gathered[a].shape[1] // 2
        c0, c1 = first[a]
        c0.wait_recv()
        f0 = remote(
            gathered[a].at[0, pl.ds(0, n)],
            gathered[a].at[2, pl.ds(0, n)],
            s_ring.at[a, 2],
            r_ring.at[a, 2],
            (d, ring_r),
        )
        f0.start()
        c1.wait_recv()
        f1 = remote(
            gathered[a].at[1, pl.ds(n, n)],
            gathered[a].at[2, pl.ds(n, n)],
            s_ring.at[a, 3],
            r_ring.at[a, 3],
            (d, ring_l),
        )
        f1.start()
        second[a] = (f0, f1)

    def complete(a):
        second[a][0].wait_recv()
        second[a][1].wait_recv()

    def fetch_in(slot):
        src = mine if slot == 0 else (gate_all.at[slot - 1], up_all.at[slot - 1])
        s = slot % 2
        cs = []
        for i in range(2):
            c = pltpu.make_async_copy(
                src[i], wbuf.at[s, :, pl.ds(i * 128, 128)], w_sem.at[s, i]
            )
            c.start()
            cs.append(c)
        return cs

    def fetch_out(slot):
        src = down.at[0] if slot == 0 else down_all.at[slot - 1]
        s = slot % 2
        c = pltpu.make_async_copy(src, dbuf.at[s], w_sem.at[s, 2])
        c.start()
        return c

    for a in range(3):
        begin(a)
    in_copies = {0: fetch_in(0)}
    out_copies = {0: fetch_out(0)}

    def fill(i, carry):
        at = rows_at(i * 16, 16)
        r = lax.broadcasted_iota(I32, (16, 128), 0) + i * 16
        lane = lax.broadcasted_iota(I32, (16, 128), 1)
        outer = lax.shift_right_logical(r * 14564, 21)
        inner = r - outer * BACK
        mid = lax.shift_right_logical(inner * 6554, 16)
        back = jnp.where(inner < 140, mid * 80 + outer * CAP + inner - mid * CAP, -1)
        outer = lax.shift_right_logical(r * 26215, 21)
        inner = r - outer * 80
        mid = lax.shift_right_logical(inner * 6554, 16)
        last = inner - mid * CAP
        home = mid * BACK + outer * CAP + last
        swap = mid * 80 + outer * CAP + last
        for j in range(9):
            sl = slice(j * 128, (j + 1) * 128)
            perm_back[at, sl] = jnp.where(lane + j * 128 == back, 1.0, 0.0).astype(BF)
            perm_home[at, sl] = jnp.where(lane + j * 128 == home, 1.0, 0.0).astype(BF)

        @pl.when(i < 40)
        def _():
            for j in range(5):
                sl = slice(j * 128, (j + 1) * 128)
                perm[at, sl] = jnp.where(lane + j * 128 == swap, 1.0, 0.0).astype(BF)

        return carry

    lax.fori_loop(0, 72, fill, 0)
    pile[1120:1152, :] = jnp.zeros((32, UNIT), BF)
    gains[...] = gain[...].astype(F32)

    names = lax.broadcasted_iota(I32, (EXPERTS, TOK), 0)
    named = [names == ids[m : m + 1, :] for m in range(2)]
    uses = jnp.where(jnp.logical_or(named[0], named[1]), 1.0, 0.0).astype(BF)
    t0 = lax.broadcasted_iota(I32, (TOK, TOK), 0)
    t1 = lax.broadcasted_iota(I32, (TOK, TOK), 1)
    eye = jnp.where(t0 == t1, 1.0, 0.0).astype(BF)
    earlier = jnp.dot(uses, jnp.where(t0 < t1, 1.0, 0.0).astype(BF), preferred_element_type=F32)
    step = (rem(div(names, 2), 8) - rem(div(d, 2), 8) + 8) % 8
    order = jnp.where(step > 4, 16 - 2 * step, jnp.maximum(2 * step - 1, 0))
    ahead = (
        (div(names, 16) - div(d, 16) + 2) % 2 * 16
        + order * 2
        + (rem(names, 2) - rem(d, 2) + 2) % 2
    )
    table = ahead.astype(F32) * CAP + earlier
    pos = [
        jnp.sum(jnp.where(named[m], table, 0.0), axis=0, keepdims=True).astype(I32)
        for m in range(2)
    ]

    for c in attn_out[:15]:
        c.wait_recv()
    own_cols.wait()
    own_res.wait()

    def add_cols(i, total):
        at = lanes_at(i * UNIT, UNIT)
        s = normed[:, at].astype(F32) + nt_dot(eye, cols[rows_at(i * UNIT, UNIT), :])
        stream[:, at] = s
        sq = s * s
        return total + sq[:, 0:128] + sq[:, 128:256]

    near = div(d, 16) * 14
    total = lax.fori_loop(near, near + 14, add_cols, jnp.zeros((TOK, 128), F32))
    for c in attn_out[15:]:
        c.wait_recv()
    pass_on(0)
    total = lax.fori_loop(14 - near, 28 - near, add_cols, total)
    inv = lax.rsqrt(jnp.sum(total, axis=1, keepdims=True) * (1.0 / D) + 1e-06)

    def scale_cols(i, carry):
        at = lanes_at(i * 128, 128)
        normed[:, at] = (stream[:, at] * inv * gains[pl.ds(i, 1), :]).astype(BF)
        return carry

    lax.fori_loop(0, D // 128, scale_cols, 0)

    def disp_copy(k):
        at = rows_at(k * 80, 80)
        return remote(
            outgoing.at[at],
            arrived.at[0, at],
            s_disp.at[k],
            r_disp.at[k],
            (shifted(d, k, 1), jnp.where(jnp.int32(k) < 16, b, other)),
        )

    def dispatch(g, carry):
        want = lax.broadcasted_iota(I32, (80, TOK), 0) + g * 80
        hit = jnp.logical_or(want == pos[0], want == pos[1])
        one = jnp.where(hit, 1.0, 0.0).astype(BF)
        for j in range(8):
            stack[j * 80 : (j + 1) * 80, :] = jnp.dot(
                one, normed[:, j * CHUNK : (j + 1) * CHUNK], preferred_element_type=F32
            ).astype(BF)
        for n in range(0, CHUNK, UNIT):
            at = slice(n, min(n + UNIT, CHUNK))
            outgoing[rows_at(g * 640, 640), at] = jnp.dot(
                perm[...], stack[:, at], preferred_element_type=F32
            ).astype(BF)
        for i in range(8):
            k = g * 8 + i

            @pl.when(jnp.logical_and(k > 0, k <= AHEAD))
            def _():
                disp_copy(k).start()

        return carry

    lax.fori_loop(0, 4, dispatch, 0)
    own_rows = pltpu.make_async_copy(
        outgoing.at[pl.ds(0, 80)], arrived.at[0, pl.ds(0, 80)], l_sem.at[2]
    )
    own_rows.start()

    logits = jnp.zeros((EXPERTS, TOK), F32)
    for q in range(8):
        sl = slice(q * CHUNK, (q + 1) * CHUNK)
        logits += nt_dot(router[:, sl], normed[:, sl])
    affinity = jax.nn.sigmoid(logits)
    chosen = [jnp.sum(jnp.where(n, affinity, 0.0), axis=0, keepdims=True) for n in named]
    scale = 2.5 / (chosen[0] + chosen[1])
    for part in range(2):
        where = lax.broadcasted_iota(I32, (160, TOK), 0) + part * 160
        full = jnp.where(where == pos[0], chosen[0] * scale, 0.0) + jnp.where(
            where == pos[1], chosen[1] * scale, 0.0
        )
        high = full.astype(BF)
        low = (full - high.astype(F32)).astype(BF)
        coef[part, 0:TOK, :] = nt_dot(eye, high).astype(BF)
        coef[part, TOK : 2 * TOK, :] = nt_dot(eye, low).astype(BF)

    def fwd_copy(k):
        at = rows_at(k * 80, 80)
        return remote(arrived.at[0, at], arrived.at[1, at], s_fwd.at[k], r_fwd.at[k], (d, other))

    def spread(side, g):
        base = (g // 2) * SLOTS + side * 160 + (g % 2) * 80
        for n in range(0, CHUNK, UNIT):
            m = min(n + UNIT, CHUNK)
            z = jnp.dot(
                perm[...], arrived[side, rows_at(g * 640, 640), n:m], preferred_element_type=F32
            ).astype(BF)
            for j in range(8):
                rows[rows_at(base, 80), j * CHUNK + n : j * CHUNK + m] = z[j * 80 : (j + 1) * 80]

    def take(first_k, n):
        for k in range(first_k, first_k + n):
            if k > 0:
                disp_copy(k).wait_recv()
            fwd_copy(k).start()
            if k > 0 and k + AHEAD < EXPERTS:
                disp_copy(k).wait_send()
                disp_copy(k + AHEAD).start()

    def arrive_other(g, carry):
        for i in range(8):
            fwd_copy(g * 8 + i).wait_recv()
        spread(1, g)
        return carry

    def project_in(batch, slot):
        at = slice(batch * SLOTS, (batch + 1) * SLOTS)
        for c in in_copies[slot]:
            c.wait()

        def step(i, carry):
            ks = pl.ds(pl.multiple_of(i * 1024, 1024), 1024)
            part = jnp.dot(rows[at, ks], wbuf[slot % 2, ks, :], preferred_element_type=F32)

            @pl.when(i == 0)
            def _():
                acc[...] = part

            @pl.when(i > 0)
            def _():
                acc[...] += part

            return carry

        lax.fori_loop(0, 7, step, 0)
        g = acc[:, 0:128]
        h = (g / (1.0 + jnp.exp(-g)) * acc[:, 128:256]).astype(BF)
        hidden[0, at, lanes_at(shard_of[slot] * 128, 128)] = h

    def swap_hidden(batch):
        cs = []
        for i in range(2):
            c = remote(
                hidden.at[0, pl.ds(batch * SLOTS + i * 160, 160)],
                hidden.at[1, pl.ds(batch * SLOTS + (1 - i) * 160, 160)],
                s_hid.at[batch, i],
                r_hid.at[batch, 1 - i],
                (d, other),
            )
            c.start()
            cs.append(c)
        return cs

    def project_out(batch):
        for slot in range(4):
            out_copies[slot].wait()
            at = slice(batch * SLOTS, (batch + 1) * SLOTS)
            for n in range(0, CHUNK, UNIT):
                w = min(UNIT, CHUNK - n)
                res = nt_dot(
                    hidden[0, at, :], dbuf[slot % 2, n : n + w, lanes_at(half * 512, 512)]
                )
                res += nt_dot(
                    hidden[1, at, :], dbuf[slot % 2, n : n + w, lanes_at(far * 512, 512)]
                )
                for side in range(2):
                    to = lanes_at(shard_of[slot] * CHUNK + side * HALF + n, w)
                    rows[batch * SLOTS : batch * SLOTS + 160, to] = res[
                        side * 160 : (side + 1) * 160
                    ].astype(BF)
            if slot == 0:
                out_copies[2] = fetch_out(2)
            elif slot == 2 and batch == 0:
                complete(2)
                out_copies[3] = fetch_out(3)
                out_copies[0] = fetch_out(0)
            elif slot == 1 and batch == 1:
                out_copies[3] = fetch_out(3)
            elif slot == 3 and batch == 0:
                out_copies[1] = fetch_out(1)

    def ret_copy(side, k):
        at = rows_at(k * BACK, BACK)
        near = jnp.where(k < 16, b, other)
        flip = jnp.where(k < 16, other, b)
        return remote(
            sending.at[side, at],
            returned.at[half, at],
            s_ret.at[side, k],
            r_ret.at[half, k],
            (shifted(d, k, -1), near if side == 0 else flip),
        )

    def ret_wait(h, k):
        at = rows_at(k * BACK, BACK)
        return remote(
            sending.at[0, at],
            returned.at[h, at],
            s_ret.at[0, k],
            r_ret.at[h, k],
            (shifted(d, k, 1), other),
        )

    def send_back(batch):
        for side in (1, 0):

            def body(g, carry, side=side):
                base = batch * SLOTS + (g - batch * 2) * 80
                for u in range(14):
                    at = side * HALF + u * UNIT
                    pile[u * 80 : (u + 1) * 80, :] = rows[rows_at(base, 80), at : at + UNIT]
                sending[side, rows_at(g * 1152, 1152), :] = jnp.dot(
                    perm_back[...], pile[...], preferred_element_type=F32
                ).astype(BF)
                for i in range(8):
                    k = g * 8 + i
                    if side == 0 and batch == 0 and i == 0:

                        @pl.when(k > 0)
                        def _():
                            ret_copy(0, k).start()
                    else:
                        ret_copy(side, k).start()
                return carry

            lax.fori_loop(2 * batch, 2 * batch + 2, body, 0)

    def home(batch):
        for h in range(2):

            def body(g, carry, h=h):
                for i in range(8):
                    k = g * 8 + i
                    if batch == 0 and i == 0:

                        @pl.when(jnp.logical_or(k > 0, half != h))
                        def _():
                            ret_wait(h, k).wait_recv()
                    else:
                        ret_wait(h, k).wait_recv()
                z = jnp.dot(
                    perm_home[0:1120, :],
                    returned[h, rows_at(g * 1152, 1152), :],
                    preferred_element_type=F32,
                ).astype(BF)
                base = batch * SLOTS + 160 + (g - 2 * batch) * 80
                for u in range(14):
                    at = h * HALF + u * UNIT
                    rows[rows_at(base, 80), at : at + UNIT] = z[u * 80 : (u + 1) * 80, :]
                return carry

            lax.fori_loop(2 * batch, 2 * batch + 2, body, 0)

    def combine(batch):
        def body(i, carry):
            at = lanes_at(i * 512, 512)
            both = jnp.dot(
                coef[batch],
                rows[batch * SLOTS + 160 : (batch + 1) * SLOTS, at],
                preferred_element_type=F32,
            )
            s = stream[:, at] + both[0:TOK, :] + both[TOK : 2 * TOK, :]
            if batch == 0:
                stream[:, at] = s
            else:
                normed[:, at] = s.astype(BF)
            return carry

        lax.fori_loop(0, D // 512, body, 0)

    own_rows.wait()
    take(0, 8)
    pass_on(1)
    in_copies[1] = fetch_in(1)
    spread(0, 0)
    take(8, 8)
    spread(0, 1)
    take(16, 2)
    arrive_other(0, 0)
    take(18, 2)
    arrive_other(1, 0)
    pass_on(2)
    out_copies[1] = fetch_out(1)
    project_in(0, 0)
    in_copies[2] = fetch_in(2)
    project_in(0, 1)
    project_in(0, 2)
    in_copies[0] = fetch_in(0)
    take(20, 4)
    complete(0)
    complete(1)
    in_copies[3] = fetch_in(3)
    spread(0, 2)
    project_in(0, 3)
    in_copies[1] = fetch_in(1)
    hid_a = swap_hidden(0)
    take(24, 8)
    spread(0, 3)
    for c in hid_a:
        c.wait_recv()
    project_out(0)
    send_back(0)
    own_back = pltpu.make_async_copy(
        sending.at[0, pl.ds(0, BACK)], returned.at[half, pl.ds(0, BACK)], l_sem.at[3]
    )
    own_back.start()
    lax.fori_loop(2, 4, arrive_other, 0)
    project_in(1, 0)
    in_copies[2] = fetch_in(2)
    project_in(1, 1)
    in_copies[3] = fetch_in(3)
    project_in(1, 2)
    project_in(1, 3)
    hid_b = swap_hidden(1)
    for c in hid_b:
        c.wait_recv()
    project_out(1)
    send_back(1)
    own_back.wait()
    home(0)
    combine(0)
    home(1)
    combine(1)
    result = pltpu.make_async_copy(normed, out, l_sem.at[4])
    result.start()

    for c in attn_out:
        c.wait_send()
    for a in range(3):
        for c in first[a] + second[a]:
            c.wait_send()
    for c in hid_a + hid_b:
        c.wait_send()

    def drain(k, carry):
        @pl.when(k > 0)
        def _():
            ret_copy(0, k).wait_send()

        @pl.when(k >= EXPERTS - AHEAD)
        def _():
            disp_copy(k).wait_send()

        fwd_copy(k).wait_send()
        ret_copy(1, k).wait_send()
        return carry

    lax.fori_loop(0, EXPERTS, drain, 0)
    result.wait()


def layer(attn, residual, gain, router, ids, gate, up, down):
    any_ = pl.BlockSpec(memory_space=pl.ANY)
    vmem = pl.BlockSpec(memory_space=pltpu.VMEM)
    dma = pltpu.SemaphoreType.DMA
    got = pl.pallas_call(
        kernel,
        out_shape=[
            jax.ShapeDtypeStruct((TOK, D), BF),
            jax.ShapeDtypeStruct((3, D, 128), BF),
            jax.ShapeDtypeStruct((3, D, 128), BF),
            jax.ShapeDtypeStruct((3, CHUNK, FF), BF),
        ],
        in_specs=[any_, any_, vmem, vmem, vmem, any_, any_, any_],
        out_specs=[any_] * 4,
        scratch_shapes=[
            pltpu.VMEM((D, TOK), BF),
            pltpu.VMEM((TOK, D), F32),
            pltpu.VMEM((TOK, D), BF),
            pltpu.VMEM((56, 128), F32),
            pltpu.VMEM((640, 640), BF),
            pltpu.VMEM((1152, 1152), BF),
            pltpu.VMEM((1152, 1152), BF),
            pltpu.VMEM((640, CHUNK), BF),
            pltpu.VMEM((2560, CHUNK), BF),
            pltpu.VMEM((2, 2560, CHUNK), BF),
            pltpu.VMEM((2 * SLOTS, D), BF),
            pltpu.VMEM((2, D, UNIT), BF),
            pltpu.VMEM((2, CHUNK, FF), BF),
            pltpu.VMEM((SLOTS, UNIT), F32),
            pltpu.VMEM((2, 2 * SLOTS, FF // 2), BF),
            pltpu.VMEM((1152, UNIT), BF),
            pltpu.VMEM((2, 32 * BACK, UNIT), BF),
            pltpu.VMEM((2, 32 * BACK, UNIT), BF),
            pltpu.VMEM((2, 2 * TOK, 160), BF),
            dma((32,)),
            dma((32,)),
            dma((3, 4)),
            dma((3, 4)),
            dma((32,)),
            dma((32,)),
            dma((32,)),
            dma((32,)),
            dma((2, 2)),
            dma((2, 2)),
            dma((2, 32)),
            dma((2, 32)),
            dma((5,)),
            dma((2, 3)),
        ],
        compiler_params=pltpu.CompilerParams(
            collective_id=0, has_side_effects=True, vmem_limit_bytes=64 * 1024 * 1024 - 4096
        ),
        cost_estimate=pl.CostEstimate(
            flops=20_000_000_000, bytes_accessed=80_000_000, transcendentals=400_000
        ),
    )(attn, residual, gain, router, ids, gate, up, down)
    return got[0]


def body(
    attn_cols, residual, norm_gain, router_weight, expert_ids, gate_weight, up_weight, down_weight
):
    return layer(
        attn_cols.T,
        residual,
        norm_gain.reshape(D // 128, 128),
        router_weight.T,
        expert_ids.T,
        gate_weight,
        up_weight,
        down_weight,
    )


def solution(mesh):
    return jax.shard_map(
        body,
        mesh=mesh,
        in_specs=(
            P("blk", "dp"),
            P(("blk", "dp"), None),
            P(),
            P(),
            P(("blk", "dp"), None),
            P("dp", None, "blk"),
            P("dp", None, "blk"),
            P("dp", "blk", None),
        ),
        out_specs=P(("blk", "dp"), None),
        check_vma=False,
    )
```

```python
import jax
import jax.numpy as jnp
from jax import lax
from jax.experimental import pallas as pl
from jax.experimental.pallas import tpu as pltpu
from jax.sharding import PartitionSpec as P

BF = jnp.bfloat16
F32 = jnp.float32
I32 = jnp.int32
D = 7168
FF = 1024
TOK = 128
EXPERTS = 32
CAP = 10
SLOTS = EXPERTS * CAP
PIECE = 224
CHUNK = 896
HALF = D // 2
UNIT = 256
BACK = 144
AHEAD = 7
MESH = pl.DeviceIdType.MESH


def div(a, n):
    return lax.div(a, jnp.int32(n))


def rem(a, n):
    return lax.rem(a, jnp.int32(n))


def shifted(d, k, sign):
    x = rem(div(d, 16) + k // 16, 2)
    i = (k // 2) % 8
    step = (i % 2) * ((i + 1) // 2) + (1 - i % 2) * ((8 - i // 2) % 8)
    z = rem(rem(div(d, 2), 8) + (sign * step + 8), 8)
    c = rem(rem(d, 2) + k % 2, 2)
    return x * 16 + z * 2 + c


def nt_dot(a, b):
    return lax.dot_general(a, b, (((1,), (1,)), ((), ())), preferred_element_type=F32)


def rows_at(start, n):
    return pl.ds(pl.multiple_of(start, 16), n)


def kernel(
    attn,
    residual,
    gain,
    router,
    ids,
    gate,
    up,
    down,
    out,
    gate_all,
    up_all,
    down_all,
    cols,
    stream,
    normed,
    gains,
    perm,
    perm_back,
    perm_home,
    stack,
    outgoing,
    arrived,
    rows,
    wbuf,
    dbuf,
    acc,
    hidden,
    pile,
    sending,
    returned,
    coef,
    s_attn,
    r_attn,
    s_ring,
    r_ring,
    s_disp,
    r_disp,
    s_fwd,
    r_fwd,
    s_hid,
    r_hid,
    s_ret,
    r_ret,
    l_sem,
    w_sem,
):
    d = lax.axis_index("dp")
    b = lax.axis_index("blk")
    other = rem(b + 4, 8)
    half = div(b, 4)
    far = 1 - half
    y = rem(b, 4)
    ring_r = half * 4 + rem(y + 1, 4)
    ring_l = half * 4 + rem(y + 3, 4)
    shard_of = (y, rem(y + 3, 4), rem(y + 1, 4), rem(y + 2, 4))

    def remote(src, dst, ss, rs, dev):
        return pltpu.make_async_remote_copy(
            src_ref=src,
            dst_ref=dst,
            send_sem=ss,
            recv_sem=rs,
            device_id=dev,
            device_id_type=MESH,
        )

    def lanes_at(start, n):
        return pl.ds(pl.multiple_of(start, 128), n)

    own_cols = pltpu.make_async_copy(
        attn.at[:, lanes_at(d * TOK, TOK)], cols.at[rows_at(d * PIECE, PIECE)], l_sem.at[0]
    )
    own_cols.start()
    own_res = pltpu.make_async_copy(residual, normed, l_sem.at[1])
    own_res.start()

    barrier = pltpu.get_barrier_semaphore()
    for k in range(EXPERTS):
        p = shifted(d, k, 1)
        for q in (b, other):
            if k == 0 and q is b:
                continue
            pl.semaphore_signal(barrier, inc=1, device_id=(p, q), device_id_type=MESH)
    for q in (ring_l, ring_r):
        pl.semaphore_signal(barrier, inc=1, device_id=(d, q), device_id_type=MESH)
    pl.semaphore_wait(barrier, 65)

    attn_out = []
    for k in range(1, 32):
        p = shifted(d, k, 1)
        c = remote(
            attn.at[:, lanes_at(p * TOK, TOK)],
            cols.at[rows_at(d * PIECE, PIECE)],
            s_attn.at[k],
            r_attn.at[k],
            (p, b),
        )
        c.start()
        attn_out.append(c)

    mine = (gate.at[0], up.at[0], down.at[0])
    gathered = (gate_all, up_all, down_all)
    first = {}
    second = {}

    def begin(a):
        c0 = remote(mine[a], gathered[a].at[0], s_ring.at[a, 0], r_ring.at[a, 0], (d, ring_r))
        c1 = remote(mine[a], gathered[a].at[1], s_ring.at[a, 1], r_ring.at[a, 1], (d, ring_l))
        c0.start()
        c1.start()
        first[a] = (c0, c1)

    def pass_on(a):
        n = gathered[a].shape[1] // 2
        c0, c1 = first[a]
        c0.wait_recv()
        f0 = remote(
            gathered[a].at[0, pl.ds(0, n)],
            gathered[a].at[2, pl.ds(0, n)],
            s_ring.at[a, 2],
            r_ring.at[a, 2],
            (d, ring_r),
        )
        f0.start()
        c1.wait_recv()
        f1 = remote(
            gathered[a].at[1, pl.ds(n, n)],
            gathered[a].at[2, pl.ds(n, n)],
            s_ring.at[a, 3],
            r_ring.at[a, 3],
            (d, ring_l),
        )
        f1.start()
        second[a] = (f0, f1)

    def complete(a):
        second[a][0].wait_recv()
        second[a][1].wait_recv()

    def fetch_in(slot):
        src = mine if slot == 0 else (gate_all.at[slot - 1], up_all.at[slot - 1])
        s = slot % 2
        cs = []
        for i in range(2):
            c = pltpu.make_async_copy(
                src[i], wbuf.at[s, :, pl.ds(i * 128, 128)], w_sem.at[s, i]
            )
            c.start()
            cs.append(c)
        return cs

    def fetch_out(slot):
        src = down.at[0] if slot == 0 else down_all.at[slot - 1]
        s = slot % 2
        c = pltpu.make_async_copy(src, dbuf.at[s], w_sem.at[s, 2])
        c.start()
        return c

    for a in range(3):
        begin(a)
    in_copies = {0: fetch_in(0)}
    out_copies = {0: fetch_out(0)}

    def fill(i, carry):
        at = rows_at(i * 16, 16)
        r = lax.broadcasted_iota(I32, (16, 128), 0) + i * 16
        lane = lax.broadcasted_iota(I32, (16, 128), 1)
        outer = lax.shift_right_logical(r * 14564, 21)
        inner = r - outer * BACK
        mid = lax.shift_right_logical(inner * 6554, 16)
        back = jnp.where(inner < 140, mid * 80 + outer * CAP + inner - mid * CAP, -1)
        outer = lax.shift_right_logical(r * 26215, 21)
        inner = r - outer * 80
        mid = lax.shift_right_logical(inner * 6554, 16)
        last = inner - mid * CAP
        home = mid * BACK + outer * CAP + last
        swap = mid * 80 + outer * CAP + last
        for j in range(9):
            sl = slice(j * 128, (j + 1) * 128)
            perm_back[at, sl] = jnp.where(lane + j * 128 == back, 1.0, 0.0).astype(BF)
            perm_home[at, sl] = jnp.where(lane + j * 128 == home, 1.0, 0.0).astype(BF)

        @pl.when(i < 40)
        def _():
            for j in range(5):
                sl = slice(j * 128, (j + 1) * 128)
                perm[at, sl] = jnp.where(lane + j * 128 == swap, 1.0, 0.0).astype(BF)

        return carry

    lax.fori_loop(0, 72, fill, 0)
    pile[1120:1152, :] = jnp.zeros((32, UNIT), BF)
    gains[...] = gain[...].astype(F32)

    names = lax.broadcasted_iota(I32, (EXPERTS, TOK), 0)
    named = [names == ids[m : m + 1, :] for m in range(2)]
    uses = jnp.where(jnp.logical_or(named[0], named[1]), 1.0, 0.0).astype(BF)
    t0 = lax.broadcasted_iota(I32, (TOK, TOK), 0)
    t1 = lax.broadcasted_iota(I32, (TOK, TOK), 1)
    eye = jnp.where(t0 == t1, 1.0, 0.0).astype(BF)
    earlier = jnp.dot(uses, jnp.where(t0 < t1, 1.0, 0.0).astype(BF), preferred_element_type=F32)
    step = (rem(div(names, 2), 8) - rem(div(d, 2), 8) + 8) % 8
    order = jnp.where(step > 4, 16 - 2 * step, jnp.maximum(2 * step - 1, 0))
    ahead = (
        (div(names, 16) - div(d, 16) + 2) % 2 * 16
        + order * 2
        + (rem(names, 2) - rem(d, 2) + 2) % 2
    )
    table = ahead.astype(F32) * CAP + earlier
    pos = [
        jnp.sum(jnp.where(named[m], table, 0.0), axis=0, keepdims=True).astype(I32)
        for m in range(2)
    ]

    for c in attn_out[:15]:
        c.wait_recv()
    own_cols.wait()
    own_res.wait()

    def add_cols(i, total):
        at = lanes_at(i * UNIT, UNIT)
        s = normed[:, at].astype(F32) + nt_dot(eye, cols[rows_at(i * UNIT, UNIT), :])
        stream[:, at] = s
        sq = s * s
        return total + sq[:, 0:128] + sq[:, 128:256]

    near = div(d, 16) * 14
    total = lax.fori_loop(near, near + 14, add_cols, jnp.zeros((TOK, 128), F32))
    for c in attn_out[15:]:
        c.wait_recv()
    pass_on(0)
    total = lax.fori_loop(14 - near, 28 - near, add_cols, total)
    inv = lax.rsqrt(jnp.sum(total, axis=1, keepdims=True) * (1.0 / D) + 1e-06)

    def scale_cols(i, carry):
        at = lanes_at(i * 128, 128)
        normed[:, at] = (stream[:, at] * inv * gains[pl.ds(i, 1), :]).astype(BF)
        return carry

    lax.fori_loop(0, D // 128, scale_cols, 0)

    def disp_copy(k):
        at = rows_at(k * 80, 80)
        return remote(
            outgoing.at[at],
            arrived.at[0, at],
            s_disp.at[k],
            r_disp.at[k],
            (shifted(d, k, 1), jnp.where(jnp.int32(k) < 16, b, other)),
        )

    def dispatch(g, carry):
        want = lax.broadcasted_iota(I32, (80, TOK), 0) + g * 80
        hit = jnp.logical_or(want == pos[0], want == pos[1])
        one = jnp.where(hit, 1.0, 0.0).astype(BF)
        for j in range(8):
            stack[j * 80 : (j + 1) * 80, :] = jnp.dot(
                one, normed[:, j * CHUNK : (j + 1) * CHUNK], preferred_element_type=F32
            ).astype(BF)
        for n in range(0, CHUNK, UNIT):
            at = slice(n, min(n + UNIT, CHUNK))
            outgoing[rows_at(g * 640, 640), at] = jnp.dot(
                perm[...], stack[:, at], preferred_element_type=F32
            ).astype(BF)
        for i in range(8):
            k = g * 8 + i

            @pl.when(jnp.logical_and(k > 0, k <= AHEAD))
            def _():
                disp_copy(k).start()

        return carry

    lax.fori_loop(0, 4, dispatch, 0)
    own_rows = pltpu.make_async_copy(
        outgoing.at[pl.ds(0, 80)], arrived.at[0, pl.ds(0, 80)], l_sem.at[2]
    )
    own_rows.start()

    logits = jnp.zeros((EXPERTS, TOK), F32)
    for q in range(8):
        sl = slice(q * CHUNK, (q + 1) * CHUNK)
        logits += nt_dot(router[:, sl], normed[:, sl])
    affinity = jax.nn.sigmoid(logits)
    chosen = [jnp.sum(jnp.where(n, affinity, 0.0), axis=0, keepdims=True) for n in named]
    scale = 2.5 / (chosen[0] + chosen[1])
    for part in range(2):
        where = lax.broadcasted_iota(I32, (160, TOK), 0) + part * 160
        full = jnp.where(where == pos[0], chosen[0] * scale, 0.0) + jnp.where(
            where == pos[1], chosen[1] * scale, 0.0
        )
        high = full.astype(BF)
        low = (full - high.astype(F32)).astype(BF)
        coef[part, 0:TOK, :] = nt_dot(eye, high).astype(BF)
        coef[part, TOK : 2 * TOK, :] = nt_dot(eye, low).astype(BF)

    def fwd_copy(k):
        at = rows_at(k * 80, 80)
        return remote(arrived.at[0, at], arrived.at[1, at], s_fwd.at[k], r_fwd.at[k], (d, other))

    def spread(side, g):
        base = (g // 2) * SLOTS + side * 160 + (g % 2) * 80
        for n in range(0, CHUNK, UNIT):
            m = min(n + UNIT, CHUNK)
            z = jnp.dot(
                perm[...], arrived[side, rows_at(g * 640, 640), n:m], preferred_element_type=F32
            ).astype(BF)
            for j in range(8):
                rows[rows_at(base, 80), j * CHUNK + n : j * CHUNK + m] = z[j * 80 : (j + 1) * 80]

    def take(first_k, n):
        for k in range(first_k, first_k + n):
            if k > 0:
                disp_copy(k).wait_recv()
            fwd_copy(k).start()
            if k > 0 and k + AHEAD < EXPERTS:
                disp_copy(k).wait_send()
                disp_copy(k + AHEAD).start()

    def arrive_other(g, carry):
        for i in range(8):
            fwd_copy(g * 8 + i).wait_recv()
        spread(1, g)
        return carry

    def project_in(batch, slot):
        at = slice(batch * SLOTS, (batch + 1) * SLOTS)
        for c in in_copies[slot]:
            c.wait()

        def step(i, carry):
            ks = pl.ds(pl.multiple_of(i * 1024, 1024), 1024)
            part = jnp.dot(rows[at, ks], wbuf[slot % 2, ks, :], preferred_element_type=F32)

            @pl.when(i == 0)
            def _():
                acc[...] = part

            @pl.when(i > 0)
            def _():
                acc[...] += part

            return carry

        lax.fori_loop(0, 7, step, 0)
        g = acc[:, 0:128]
        h = (g / (1.0 + jnp.exp(-g)) * acc[:, 128:256]).astype(BF)
        hidden[0, at, lanes_at(shard_of[slot] * 128, 128)] = h

    def swap_hidden(batch):
        cs = []
        for i in range(2):
            c = remote(
                hidden.at[0, pl.ds(batch * SLOTS + i * 160, 160)],
                hidden.at[1, pl.ds(batch * SLOTS + (1 - i) * 160, 160)],
                s_hid.at[batch, i],
                r_hid.at[batch, 1 - i],
                (d, other),
            )
            c.start()
            cs.append(c)
        return cs

    def project_out(batch, slots):
        for slot in slots:
            out_copies[slot].wait()
            at = slice(batch * SLOTS, (batch + 1) * SLOTS)
            for n in range(0, CHUNK, UNIT):
                w = min(UNIT, CHUNK - n)
                res = nt_dot(
                    hidden[0, at, :], dbuf[slot % 2, n : n + w, lanes_at(half * 512, 512)]
                )
                res += nt_dot(
                    hidden[1, at, :], dbuf[slot % 2, n : n + w, lanes_at(far * 512, 512)]
                )
                for side in range(2):
                    to = lanes_at(shard_of[slot] * CHUNK + side * HALF + n, w)
                    rows[batch * SLOTS : batch * SLOTS + 160, to] = res[
                        side * 160 : (side + 1) * 160
                    ].astype(BF)
            if slot == 0:
                out_copies[2] = fetch_out(2)
            elif slot == 2 and batch == 0:
                out_copies[0] = fetch_out(0)
            elif slot == 1 and batch == 1:
                out_copies[3] = fetch_out(3)
            elif slot == 3 and batch == 0:
                out_copies[1] = fetch_out(1)

    def ret_copy(side, k):
        at = rows_at(k * BACK, BACK)
        near = jnp.where(k < 16, b, other)
        flip = jnp.where(k < 16, other, b)
        return remote(
            sending.at[side, at],
            returned.at[half, at],
            s_ret.at[side, k],
            r_ret.at[half, k],
            (shifted(d, k, -1), near if side == 0 else flip),
        )

    def ret_wait(h, k):
        at = rows_at(k * BACK, BACK)
        return remote(
            sending.at[0, at],
            returned.at[h, at],
            s_ret.at[0, k],
            r_ret.at[h, k],
            (shifted(d, k, 1), other),
        )

    def send_back(batch):
        for side in (1, 0):

            def body(g, carry, side=side):
                base = batch * SLOTS + (g - batch * 2) * 80
                for u in range(14):
                    at = side * HALF + u * UNIT
                    pile[u * 80 : (u + 1) * 80, :] = rows[rows_at(base, 80), at : at + UNIT]
                sending[side, rows_at(g * 1152, 1152), :] = jnp.dot(
                    perm_back[...], pile[...], preferred_element_type=F32
                ).astype(BF)
                for i in range(8):
                    k = g * 8 + i
                    if side == 0 and batch == 0 and i == 0:

                        @pl.when(k > 0)
                        def _():
                            ret_copy(0, k).start()
                    else:
                        ret_copy(side, k).start()
                return carry

            lax.fori_loop(2 * batch, 2 * batch + 2, body, 0)

    def home(batch):
        for h in range(2):

            def body(g, carry, h=h):
                for i in range(8):
                    k = g * 8 + i
                    if batch == 0 and i == 0:

                        @pl.when(jnp.logical_or(k > 0, half != h))
                        def _():
                            ret_wait(h, k).wait_recv()
                    else:
                        ret_wait(h, k).wait_recv()
                z = jnp.dot(
                    perm_home[0:1120, :],
                    returned[h, rows_at(g * 1152, 1152), :],
                    preferred_element_type=F32,
                ).astype(BF)
                base = batch * SLOTS + 160 + (g - 2 * batch) * 80
                for u in range(14):
                    at = h * HALF + u * UNIT
                    rows[rows_at(base, 80), at : at + UNIT] = z[u * 80 : (u + 1) * 80, :]
                return carry

            lax.fori_loop(2 * batch, 2 * batch + 2, body, 0)

    def combine(batch):
        def body(i, carry):
            at = lanes_at(i * 512, 512)
            both = jnp.dot(
                coef[batch],
                rows[batch * SLOTS + 160 : (batch + 1) * SLOTS, at],
                preferred_element_type=F32,
            )
            s = stream[:, at] + both[0:TOK, :] + both[TOK : 2 * TOK, :]
            if batch == 0:
                stream[:, at] = s
            else:
                normed[:, at] = s.astype(BF)
            return carry

        lax.fori_loop(0, D // 512, body, 0)

    own_rows.wait()
    take(0, 8)
    pass_on(1)
    in_copies[1] = fetch_in(1)
    spread(0, 0)
    take(8, 8)
    spread(0, 1)
    take(16, 2)
    arrive_other(0, 0)
    take(18, 2)
    arrive_other(1, 0)
    pass_on(2)
    out_copies[1] = fetch_out(1)
    project_in(0, 0)
    in_copies[2] = fetch_in(2)
    project_in(0, 1)
    project_in(0, 2)
    in_copies[0] = fetch_in(0)
    take(20, 4)
    complete(0)
    complete(1)
    in_copies[3] = fetch_in(3)
    spread(0, 2)
    project_in(0, 3)
    in_copies[1] = fetch_in(1)
    hid_a = swap_hidden(0)
    take(24, 4)
    for c in hid_a:
        c.wait_recv()
    project_out(0, (0, 1, 2))
    take(28, 4)
    complete(2)
    out_copies[3] = fetch_out(3)
    project_out(0, (3,))
    send_back(0)
    own_back = pltpu.make_async_copy(
        sending.at[0, pl.ds(0, BACK)], returned.at[half, pl.ds(0, BACK)], l_sem.at[3]
    )
    own_back.start()
    spread(0, 3)
    lax.fori_loop(2, 4, arrive_other, 0)
    project_in(1, 0)
    in_copies[2] = fetch_in(2)
    project_in(1, 1)
    in_copies[3] = fetch_in(3)
    project_in(1, 2)
    project_in(1, 3)
    hid_b = swap_hidden(1)
    for c in hid_b:
        c.wait_recv()
    project_out(1, range(4))
    send_back(1)
    own_back.wait()
    home(0)
    combine(0)
    home(1)
    combine(1)
    result = pltpu.make_async_copy(normed, out, l_sem.at[4])
    result.start()

    for c in attn_out:
        c.wait_send()
    for a in range(3):
        for c in first[a] + second[a]:
            c.wait_send()
    for c in hid_a + hid_b:
        c.wait_send()

    def drain(k, carry):
        @pl.when(k > 0)
        def _():
            ret_copy(0, k).wait_send()

        @pl.when(k >= EXPERTS - AHEAD)
        def _():
            disp_copy(k).wait_send()

        fwd_copy(k).wait_send()
        ret_copy(1, k).wait_send()
        return carry

    lax.fori_loop(0, EXPERTS, drain, 0)
    result.wait()


def layer(attn, residual, gain, router, ids, gate, up, down):
    any_ = pl.BlockSpec(memory_space=pl.ANY)
    vmem = pl.BlockSpec(memory_space=pltpu.VMEM)
    dma = pltpu.SemaphoreType.DMA
    got = pl.pallas_call(
        kernel,
        out_shape=[
            jax.ShapeDtypeStruct((TOK, D), BF),
            jax.ShapeDtypeStruct((3, D, 128), BF),
            jax.ShapeDtypeStruct((3, D, 128), BF),
            jax.ShapeDtypeStruct((3, CHUNK, FF), BF),
        ],
        in_specs=[any_, any_, vmem, vmem, vmem, any_, any_, any_],
        out_specs=[any_] * 4,
        scratch_shapes=[
            pltpu.VMEM((D, TOK), BF),
            pltpu.VMEM((TOK, D), F32),
            pltpu.VMEM((TOK, D), BF),
            pltpu.VMEM((56, 128), F32),
            pltpu.VMEM((640, 640), BF),
            pltpu.VMEM((1152, 1152), BF),
            pltpu.VMEM((1152, 1152), BF),
            pltpu.VMEM((640, CHUNK), BF),
            pltpu.VMEM((2560, CHUNK), BF),
            pltpu.VMEM((2, 2560, CHUNK), BF),
            pltpu.VMEM((2 * SLOTS, D), BF),
            pltpu.VMEM((2, D, UNIT), BF),
            pltpu.VMEM((2, CHUNK, FF), BF),
            pltpu.VMEM((SLOTS, UNIT), F32),
            pltpu.VMEM((2, 2 * SLOTS, FF // 2), BF),
            pltpu.VMEM((1152, UNIT), BF),
            pltpu.VMEM((2, 32 * BACK, UNIT), BF),
            pltpu.VMEM((2, 32 * BACK, UNIT), BF),
            pltpu.VMEM((2, 2 * TOK, 160), BF),
            dma((32,)),
            dma((32,)),
            dma((3, 4)),
            dma((3, 4)),
            dma((32,)),
            dma((32,)),
            dma((32,)),
            dma((32,)),
            dma((2, 2)),
            dma((2, 2)),
            dma((2, 32)),
            dma((2, 32)),
            dma((5,)),
            dma((2, 3)),
        ],
        compiler_params=pltpu.CompilerParams(
            collective_id=0, has_side_effects=True, vmem_limit_bytes=64 * 1024 * 1024 - 4096
        ),
        cost_estimate=pl.CostEstimate(
            flops=20_000_000_000, bytes_accessed=80_000_000, transcendentals=400_000
        ),
    )(attn, residual, gain, router, ids, gate, up, down)
    return got[0]


def body(
    attn_cols, residual, norm_gain, router_weight, expert_ids, gate_weight, up_weight, down_weight
):
    return layer(
        attn_cols.T,
        residual,
        norm_gain.reshape(D // 128, 128),
        router_weight.T,
        expert_ids.T,
        gate_weight,
        up_weight,
        down_weight,
    )


def solution(mesh):
    return jax.shard_map(
        body,
        mesh=mesh,
        in_specs=(
            P("blk", "dp"),
            P(("blk", "dp"), None),
            P(),
            P(),
            P(("blk", "dp"), None),
            P("dp", None, "blk"),
            P("dp", None, "blk"),
            P("dp", "blk", None),
        ),
        out_specs=P(("blk", "dp"), None),
        check_vma=False,
    )
```
